128 devices in a mesh: sec: 2 (over core), lon: 32 (over z_lo, y, x), lat: 2 (over z_hi).
Axes of the slice: x: 4, y: 4, z: 4 (z_hi: 2, z_lo: 2; z = z_hi * 2 + z_lo), core: 2. Of those that a mesh axis runs over, the one named last changes fastest.
Arguments:
- atm_state: bfloat16 [4096, 256, 256], P(('sec', 'lon', 'lat')), may hold values from -6 to 6
- cost_class: int32 [4096], P(('sec', 'lon', 'lat')), may hold values from 1 to 8, as said below
- w_in: bfloat16 [384, 256], replicated, may hold values from -0.375 to 0.375
- w_out: bfloat16 [256, 384], replicated, may hold values from -0.3125 to 0.3125
- w_flux: bfloat16 [4, 256], replicated, may hold values from -0.375 to 0.375
- feeding_block_index: int32 [16, 64, 4], P('lat', ('sec', 'lon')), may hold values from 0 to 4095, as said below
- pairwise_remap_weight: bfloat16 [16, 64, 4, 256, 256], P('lat', ('sec', 'lon')), may hold values from -0.1875 to 0.1875
- ocean_tracers: float32 [2, 40, 16, 16384], P(None, None, 'lat', ('sec', 'lon')), may hold values from -6 to 6
- land_sea: int32 [16, 16384], P('lat', ('sec', 'lon')), may hold values 0 or 1
Outputs:
- column_state_next: bfloat16 [4096, 256, 256], P(('sec', 'lon', 'lat'))
- tracer_fields_next: float32 [2, 40, 16, 16384], P(None, None, 'lat', ('sec', 'lon'))
- atmos_surface_temp: float32 [4096, 256], P(('sec', 'lon', 'lat'))
The draws below stay inside these ranges and needn't reach their ends.
Inputs may be any that keep to these rules, and one draw needn't show every extreme that they name: `cost_class`: all 32 blocks of one device share one class; among devices that differ only in their lon index, 16 hold class 1, 8 class 2 and 8 class 8. `feeding_block_index`: entry [r, c, k] is ((s * 32 + q) * 2 + t) * 32 + l with t = r // 8, s = c // 32, l = c % 32 and some q below 32; every atmosphere block is named exactly once.
All inputs are finite; a program needn't handle non-finite values. No bound on the sum of `land_sea` on one device may be relied on, other than what follows from the above.
Results may differ from the reference program's by a relative error of at most 0.013.
Values may be sent and summed in bfloat16 or wider, within the bound.
A program may use at most 64 MiB of HBM per device.

```python
import jax
import jax.numpy as jnp
from jax import lax

FEAT = 256
HID = 384
OLEV = 40
BLOCK_CELLS = 256
NREMAP = 4
OCY = 8
ATM_BLK_DEV = 32
ATMOS_BLOCKS = 4096
OCEAN_ROWS = 16
OCEAN_ROW_BLOCKS = 64
OX = 16384
N_SEC = 2
N_LON = 32
N_LAT = 2


def draw_cost_class(key, part):
    key = jax.random.fold_in(key, 5)
    subkeys = jax.random.split(key, N_SEC * N_LAT)
    shuffled = jax.vmap(lambda subkey: jax.random.permutation(subkey, N_LON))(subkeys)
    shuffled = shuffled.reshape(N_SEC, N_LAT, N_LON).transpose(0, 2, 1).astype(jnp.int32)
    quarter = shuffled // (N_LON // 4)
    classes = jnp.where(quarter < 2, 1, jnp.where(quarter == 2, 2, 8)).astype(jnp.int32)
    classes = jnp.broadcast_to(classes[:, :, :, None], (N_SEC, N_LON, N_LAT, ATM_BLK_DEV))
    return classes.reshape(-1).astype(jnp.int32)


def draw_feeding_block_index(key, part):
    key = jax.random.fold_in(key, 9)
    device_count = N_SEC * N_LON * N_LAT
    subkeys = jax.random.split(key, device_count)
    shuffled = jax.vmap(lambda subkey: jax.random.permutation(subkey, ATM_BLK_DEV))(subkeys)
    shuffled = shuffled.reshape(N_SEC, N_LON, N_LAT, OCY, NREMAP).astype(jnp.int32)
    per_peer = ATM_BLK_DEV // N_LON
    source_lon = shuffled // per_peer
    within = shuffled % per_peer
    sec_index = jnp.arange(N_SEC, dtype=jnp.int32)[:, None, None, None, None]
    lon_index = jnp.arange(N_LON, dtype=jnp.int32)[None, :, None, None, None]
    lat_index = jnp.arange(N_LAT, dtype=jnp.int32)[None, None, :, None, None]
    device = (sec_index * N_LON + source_lon) * N_LAT + lat_index
    atm_block = device * ATM_BLK_DEV + lon_index * per_peer + within
    return atm_block.transpose(2, 3, 0, 1, 4).reshape(N_LAT * OCY, N_SEC * N_LON, NREMAP).astype(jnp.int32)


def touch_ends(values, rng, least, top_value):
    longest = values.shape.index(max(values.shape))
    spots = []
    for shift in (0, 1):
        where = [jax.random.randint(jax.random.fold_in(rng, axis), (), 0, length) for axis, length in enumerate(values.shape)]
        where[longest] = (where[longest] + shift) % values.shape[longest]
        spots.append(tuple(where))
    return values.at[spots[0]].set(least).at[spots[1]].set(top_value)


def level_of(own_key, extent, pieces, least, top_value):
    def one(axis_at, parts):
        steps = jax.random.uniform(jax.random.fold_in(jax.random.fold_in(own_key, 6), axis_at), (parts,), jnp.float32, least / len(pieces), top_value / len(pieces))
        return jnp.repeat(jnp.exp(steps), extent[axis_at] // parts).reshape((-1,) + (1,) * (len(extent) - axis_at - 1))

    factor_of = one(*pieces[0])
    for cut in pieces[1:]:
        factor_of = factor_of * one(*cut)
    return factor_of


def normal_values(stream_key, dims, scale, reach, shards=(), kind=jnp.bfloat16):
    drawn = jax.random.normal(stream_key, dims, jnp.float32) * scale
    if len(shards) > 0:
        drawn = level_of(stream_key, dims, shards, -0.22, 0.18) * drawn
    return jnp.clip(drawn, min=-reach, max=reach).astype(kind)


def setup_inputs(seed: int = 0) -> dict:
    splits = jax.random.split(jax.random.key(seed), 10)
    atm_state = normal_values(splits[0], (ATMOS_BLOCKS, FEAT, BLOCK_CELLS), 1.0, 6.0, ((0, 128),))
    cost_class = draw_cost_class(jax.random.fold_in(splits[9], 71), 0)
    w_in = normal_values(splits[2], (HID, FEAT), FEAT ** -0.5, 0.375)
    w_out = normal_values(splits[3], (FEAT, HID), HID ** -0.5, 0.3125)
    w_flux = normal_values(splits[4], (4, FEAT), FEAT ** -0.5, 0.375)
    feeding_block_index = draw_feeding_block_index(jax.random.fold_in(splits[9], 71), 0)
    pairwise_remap_weight = normal_values(splits[6], (OCEAN_ROWS, OCEAN_ROW_BLOCKS, NREMAP, BLOCK_CELLS, BLOCK_CELLS), (NREMAP * BLOCK_CELLS) ** -0.5, 0.1875, ((0, 2), (1, 64)))
    ocean_tracers = normal_values(splits[7], (2, OLEV, OCEAN_ROWS, OX), 1.0, 6.0, ((2, 2), (3, 64)), jnp.float32)
    land_sea = touch_ends((jax.random.randint(splits[8], (OCEAN_ROWS, OX), 0, 4) < 3).astype(jnp.int32), jax.random.fold_in(splits[8], 1), 0, 1)
    return {"atm_state": atm_state, "cost_class": cost_class, "w_in": w_in, "w_out": w_out, "w_flux": w_flux, "feeding_block_index": feeding_block_index, "pairwise_remap_weight": pairwise_remap_weight, "ocean_tracers": ocean_tracers, "land_sea": land_sea}


def column_update(current, w_in, w_out):
    hidden = jnp.einsum('hf,bfc->bhc', w_in.astype(jnp.float32), current.astype(jnp.float32))
    hidden = lax.optimization_barrier(jax.nn.silu(hidden).astype(jnp.bfloat16))
    change = jnp.einsum('fh,bhc->bfc', w_out.astype(jnp.float32), hidden.astype(jnp.float32))
    return (current.astype(jnp.float32) + 0.5 * change).astype(jnp.bfloat16)


def physics(atm_state, cost_class, w_in, w_out):
    per_device = atm_state.reshape(ATMOS_BLOCKS // ATM_BLK_DEV, ATM_BLK_DEV, FEAT, BLOCK_CELLS)
    classes = cost_class.reshape(ATMOS_BLOCKS // ATM_BLK_DEV, ATM_BLK_DEV)

    def device_work(loop_operands):
        blocks, block_class = loop_operands

        def substep(counter, current):
            updated = column_update(current, w_in, w_out)
            return jnp.where((block_class > counter)[:, None, None], updated, current)

        return lax.fori_loop(jnp.int32(0), jnp.max(block_class), substep, blocks)

    return lax.map(device_work, (per_device, classes)).reshape(ATMOS_BLOCKS, FEAT, BLOCK_CELLS)


def ocean_update(padded, padded_mask, tracers, mask, forcing):
    levels = tracers.shape[1]
    row_count = tracers.shape[2]
    col_count = tracers.shape[3]
    spread = jnp.zeros_like(tracers)
    for row_shift, col_shift in ((0, 1), (2, 1), (1, 0), (1, 2)):
        neighbour = padded[:, :, row_shift:row_shift + row_count, col_shift:col_shift + col_count]
        near_mask = padded_mask[row_shift:row_shift + row_count, col_shift:col_shift + col_count]
        spread = spread + near_mask * (neighbour - tracers)
    wind_stress = forcing[3]
    top_mixing = 0.1 + 0.3 * wind_stress * wind_stress / (1.0 + wind_stress * wind_stress)
    mixing = jnp.concatenate([top_mixing[None], jnp.full((levels - 2, row_count, col_count), 0.1, jnp.float32)], 0)
    vertical_flux = mixing[None] * (tracers[:, 1:] - tracers[:, :-1])
    zero_layer = jnp.zeros((2, 1, row_count, col_count), jnp.float32)
    vertical = jnp.concatenate([vertical_flux, zero_layer], 1) - jnp.concatenate([zero_layer, vertical_flux], 1)
    depth_index = jnp.arange(levels, dtype=jnp.float32)
    fraction = jnp.exp(-depth_index / 8.0) - jnp.exp(-(depth_index + 1.0) / 8.0)
    surface = (depth_index == 0.0).astype(jnp.float32)
    heating = 0.5 * (forcing[1][None] * fraction[:, None, None] + forcing[0][None] * surface[:, None, None])
    freshening = 0.3 * forcing[2][None] * surface[:, None, None]
    source = jnp.stack([heating, freshening], 0)
    return tracers + mask * (0.2 * spread + vertical + source)


def reference(atm_state, cost_class, w_in, w_out, w_flux, feeding_block_index, pairwise_remap_weight, ocean_tracers, land_sea):
    column_state_next = physics(atm_state, cost_class, w_in, w_out)
    fluxes = jnp.einsum('gf,bfc->bgc', w_flux.astype(jnp.float32), column_state_next.astype(jnp.float32)).astype(jnp.bfloat16)
    flux_wide = lax.optimization_barrier(fluxes).astype(jnp.float32)

    def row_remap(loop_operands):
        index_row, weight_for_row = loop_operands
        picked = flux_wide[index_row]
        return jnp.einsum('ckgx,ckxy->cgy', picked, weight_for_row.astype(jnp.float32))

    ocean_blocks = lax.map(row_remap, (feeding_block_index, pairwise_remap_weight))
    ocean_flux = ocean_blocks.transpose(2, 0, 1, 3).reshape(4, OCEAN_ROWS, OX)
    mask = land_sea.astype(jnp.float32)
    padded = jnp.pad(ocean_tracers, ((0, 0), (0, 0), (1, 1), (1, 1)))
    padded_mask = jnp.pad(mask, 1)
    tracer_fields_next = ocean_update(padded, padded_mask, ocean_tracers, mask, ocean_flux)
    surface_temp = lax.optimization_barrier(tracer_fields_next[0, 0].astype(jnp.bfloat16))
    surface_temp_blocks = surface_temp.astype(jnp.float32).reshape(OCEAN_ROWS, OCEAN_ROW_BLOCKS, BLOCK_CELLS)

    def row_returned_home(loop_operands):
        weight_for_row, surface_temp_row = loop_operands
        return jnp.einsum('gtpr,gr->gtp', weight_for_row.astype(jnp.float32), surface_temp_row)

    weighted_terms = lax.map(row_returned_home, (pairwise_remap_weight, surface_temp_blocks))
    atmos_surface_temp = jnp.zeros((ATMOS_BLOCKS, BLOCK_CELLS), jnp.float32).at[feeding_block_index.reshape(-1)].add(weighted_terms.reshape(-1, BLOCK_CELLS))
    return (column_state_next, tracer_fields_next, atmos_surface_temp)
```

```python
import functools

import jax
import jax.numpy as jnp
import numpy as np
from jax import lax
from jax.experimental import pallas as pl
from jax.experimental.pallas import tpu as pltpu
from jax.sharding import PartitionSpec as P

F32 = jnp.float32
BF16 = jnp.bfloat16
MESH = pl.DeviceIdType.MESH


def dot(a, b):
    return jnp.dot(a, b, preferred_element_type=F32)


def contract(a, b, dim_a, dim_b):
    return lax.dot_general(
        a, b, (((dim_a,), (dim_b,)), ((), ())), preferred_element_type=F32
    )


def silu_of_half(z):
    return (z + z * jnp.tanh(z)).astype(BF16)


def physics_kernel(
    blocks, groups, cls_ref, win_ref, wout_ref, wflux_ref, x_hbm,
    y_hbm, flux_ref, xv, half_in, half_out, mix, in_sem, out_sem, *state
):
    zs, ss, hs = state[:blocks], state[blocks : 2 * blocks], state[2 * blocks :]
    width = blocks // groups

    def load(g):
        part = pl.ds(g * width, width)
        return pltpu.make_async_copy(x_hbm.at[part], xv.at[part], in_sem.at[g])

    def save(g):
        part = pl.ds(g * width, width)
        return pltpu.make_async_copy(xv.at[part], y_hbm.at[part], out_sem.at[g])

    for g in range(groups):
        load(g).start()
    half_in[...] = win_ref[...] * 0.5
    half_out[...] = wout_ref[...] * 0.5
    mix[...] = dot(half_in[...], half_out[...]).astype(BF16)
    for g in range(groups):
        load(g).wait()
        for i in range(g * width, (g + 1) * width):
            z = dot(half_in[...], xv[i])
            zs[i][...] = z
            h = silu_of_half(z)
            hs[i][...] = h
            ss[i][...] = h

    def update(_, carry):
        for i in range(blocks):
            z = zs[i][...] + dot(mix[...], hs[i][...])
            zs[i][...] = z
            h = silu_of_half(z)
            hs[i][...] = h
            ss[i][...] = ss[i][...] + h
        return carry

    lax.fori_loop(0, cls_ref[0] - 1, update, 0)
    for g in range(groups):
        for i in range(g * width, (g + 1) * width):
            y = (xv[i].astype(F32) + dot(half_out[...], ss[i][...])).astype(BF16)
            xv[i] = y
            flux = dot(wflux_ref[...], y)
            flux_ref[i, 0:4, :] = flux[:, :128]
            flux_ref[i, 4:8, :] = flux[:, 128:]
        save(g).start()
    for g in range(groups):
        save(g).wait()


def physics(cost_class, w_in, w_out, w_flux, atm_state):
    blocks, feat, cells = atm_state.shape
    hid = w_in.shape[0]
    groups = 4
    vmem = pl.BlockSpec(memory_space=pltpu.VMEM)
    anywhere = pl.BlockSpec(memory_space=pl.ANY)
    return pl.pallas_call(
        functools.partial(physics_kernel, blocks, groups),
        out_shape=(
            jax.ShapeDtypeStruct(atm_state.shape, BF16),
            jax.ShapeDtypeStruct((blocks, 8, 128), F32),
        ),
        in_specs=[pl.BlockSpec(memory_space=pltpu.SMEM), vmem, vmem, vmem, anywhere],
        out_specs=(anywhere, vmem),
        scratch_shapes=[
            pltpu.VMEM((blocks, feat, cells), BF16),
            pltpu.VMEM((hid, feat), BF16),
            pltpu.VMEM((feat, hid), BF16),
            pltpu.VMEM((hid, hid), BF16),
            pltpu.SemaphoreType.DMA((groups,)),
            pltpu.SemaphoreType.DMA((groups,)),
        ]
        + [pltpu.VMEM((hid, cells), F32)] * blocks
        + [pltpu.VMEM((hid, cells), BF16)] * (2 * blocks),
        compiler_params=pltpu.CompilerParams(vmem_limit_bytes=56 * 2**20),
        name="column_physics",
    )(cost_class, w_in, w_out, w_flux, atm_state)


def exchange_kernel(
    sec_count, lon_count, levels,
    index_ref, flux_hbm, weight_hbm, tracers_hbm, mask_hbm,
    next_hbm, temp_ref,
    weight, tracers, land, result, flux_in, terms, temp_out, temp_in,
    rows_bf, edge_out, west_in, east_in, halo, row_out, row_in, row_wide,
    weight_sem, tracer_sem, mask_sem, save_sem,
    flux_send, flux_recv, temp_send, temp_recv, halo_send, halo_recv,
):
    sec, lon, lat = lax.axis_index("sec"), lax.axis_index("lon"), lax.axis_index("lat")
    total = sec_count * lon_count
    place = sec * lon_count + lon
    before = lax.rem(place + total - 1, total)
    after = lax.rem(place + 1, total)
    west = (before // lon_count, lax.rem(before, lon_count), lat)
    east = (after // lon_count, lax.rem(after, lon_count), lat)
    across = (sec, lon, 1 - lat)
    ocean_rows, cells = land.shape
    pairs = ocean_rows * 4
    fields = 2 * levels
    lines = fields * ocean_rows

    weight_copies = [
        pltpu.make_async_copy(
            weight_hbm.at[pl.ds(8 * g, 8)], weight.at[pl.ds(8 * g, 8)], weight_sem.at[g]
        )
        for g in range(pairs // 8)
    ]
    tracer_copy = pltpu.make_async_copy(tracers_hbm, tracers, tracer_sem)
    mask_copy = pltpu.make_async_copy(mask_hbm, land, mask_sem)
    tracer_copy.start()
    mask_copy.start()
    for copy in weight_copies:
        copy.start()

    barrier = pltpu.get_barrier_semaphore()

    def greet(step, carry):
        peer = lax.rem(lon + step, lon_count)
        pl.semaphore_signal(barrier, inc=1, device_id=(sec, peer, lat), device_id_type=MESH)
        return carry

    for neighbour in (west, east, across):
        pl.semaphore_signal(barrier, inc=1, device_id=neighbour, device_id_type=MESH)
    lax.fori_loop(1, lon_count, greet, 0)
    pl.semaphore_wait(barrier, lon_count + 2)

    def spread_out(source, target, send_sem, recv_sem):
        def one(step, carry):
            peer = lax.rem(lon + step, lon_count)
            pltpu.make_async_remote_copy(
                src_ref=source.at[peer],
                dst_ref=target.at[lon],
                send_sem=send_sem,
                recv_sem=recv_sem,
                device_id=(sec, peer, lat),
                device_id_type=MESH,
            ).start()
            return carry

        lax.fori_loop(1, lon_count, one, 0)
        pltpu.make_async_copy(source.at[lon], target.at[lon], recv_sem).start()

    def await_bytes(ref, sem):
        pltpu.make_async_copy(ref, ref, sem).wait()

    spread_out(flux_hbm, flux_in, flux_send, flux_recv)

    tracer_copy.wait()
    mask_copy.wait()
    mask = land[...].astype(F32)
    rows_bf[0:lines, :] = tracers[...].reshape(lines, cells).astype(BF16)
    rows_bf[lines : lines + ocean_rows, :] = mask.astype(BF16)
    rows_bf[lines + ocean_rows :, :] = jnp.zeros(
        (rows_bf.shape[0] - lines - ocean_rows, cells), BF16
    )
    pick_row = lax.broadcasted_iota(jnp.int32, (16, cells), 0)
    pick_lane = lax.broadcasted_iota(jnp.int32, (16, cells), 1)
    pick = jnp.where(
        ((pick_row == 0) & (pick_lane == 0)) | ((pick_row == 1) & (pick_lane == cells - 1)), 1.0, 0.0
    ).astype(BF16)
    edge_out[...] = contract(pick, rows_bf[...], 1, 1)[:8]
    first = tracers[:, 0, :]
    last = tracers[:, ocean_rows - 1, :]
    near = jnp.where(lat == 0, last, first).astype(BF16)
    near_mask = jnp.where(lat == 0, mask[ocean_rows - 1 :], mask[:1])
    row_out[0:fields, :] = near
    row_out[fields:, :] = jnp.broadcast_to(near_mask, (row_out.shape[0] - fields, cells)).astype(
        BF16
    )

    def halo_copy(which, source, target, device):
        return pltpu.make_async_remote_copy(
            src_ref=source,
            dst_ref=target,
            send_sem=halo_send.at[which],
            recv_sem=halo_recv.at[which],
            device_id=device,
            device_id_type=MESH,
        )

    halo_copies = [
        halo_copy(0, edge_out, east_in, west),
        halo_copy(1, edge_out, west_in, east),
        halo_copy(2, row_out, row_in, across),
    ]
    for copy in halo_copies:
        copy.start()
    for copy in halo_copies:
        copy.wait_recv()

    edges = jnp.concatenate([west_in[...], east_in[...]], 0).astype(BF16)
    place_back = jnp.where(
        ((pick_row == 1) & (pick_lane == 0)) | ((pick_row == 8) & (pick_lane == cells - 1)), 1.0, 0.0
    ).astype(BF16)
    halo[...] = contract(edges, place_back, 0, 0)
    row_wide[...] = row_in[...].astype(F32)

    row_at = lax.broadcasted_iota(jnp.int32, (ocean_rows, cells), 0)
    lane_at = lax.broadcasted_iota(jnp.int32, (ocean_rows, cells), 1)
    top, bottom = row_at == 0, row_at == ocean_rows - 1
    left, right = lane_at == 0, lane_at == cells - 1

    def neighbours(value, side, line):
        return (
            jnp.where(left, side, pltpu.roll(value, 1, 1)),
            jnp.where(right, side, pltpu.roll(value, cells - 1, 1)),
            jnp.where(top, line, pltpu.roll(value, 1, 0)),
            jnp.where(bottom, line, pltpu.roll(value, ocean_rows - 1, 0)),
        )

    mask_w, mask_e, mask_n, mask_s = neighbours(
        mask, halo[lines : lines + ocean_rows, :], row_wide[fields : fields + 1, :]
    )
    mask_w = jnp.where(left & (place == 0), 0.0, mask_w) * 0.2
    mask_e = jnp.where(right & (place == total - 1), 0.0, mask_e) * 0.2
    mask_n = jnp.where(top & (lat == 0), 0.0, mask_n) * 0.2
    mask_s = jnp.where(bottom & (lat == 1), 0.0, mask_s) * 0.2
    mask_sum = mask_w + mask_e + mask_n + mask_s

    def level(field):
        return pl.ds(pl.multiple_of(field * ocean_rows, ocean_rows), ocean_rows)

    def interior(n):
        base = n * levels

        def one(k, carry):
            here, drop_above = carry
            f = base + k
            below = tracers[base + jnp.minimum(k + 1, levels - 1)]
            drop = below - here
            w, e, nn, s = neighbours(here, halo[level(f), :], row_wide[pl.ds(f, 1), :])
            change = (
                mask_w * w + mask_e * e + mask_n * nn + mask_s * s
                - mask_sum * here
                + 0.1 * (drop - drop_above)
            )
            result[f] = here + mask * change
            return below, drop

        start = tracers[base]
        lax.fori_loop(0, levels, one, (start, jnp.zeros_like(start)), unroll=4)

    interior(0)
    interior(1)

    await_bytes(flux_in, flux_recv)
    for copy in weight_copies:
        copy.wait()
    forcing = []
    for r in range(ocean_rows):
        total_flux = None
        for k in range(4):
            source = lax.rem(lax.shift_right_logical(index_ref[r, 0, k], 6), lon_count)
            tile = flux_in[source]
            lhs = jnp.concatenate([tile[0:4], tile[4:8]], 1).astype(BF16)
            part = dot(lhs, weight[4 * r + k])
            total_flux = part if total_flux is None else total_flux + part
        forcing.append(total_flux)
    flux_of = [
        jnp.concatenate([forcing[r][f : f + 1] for r in range(ocean_rows)], 0) for f in range(4)
    ]

    square = flux_of[3] * flux_of[3]
    extra = mask * (0.3 * square / (1.0 + square))
    decay = [float(v) for v in depth_fractions(levels)]
    heat = 0.5 * mask * flux_of[1]
    for n in range(2):
        base = n * levels
        jump = extra * (tracers[base + 1] - tracers[base])
        surface = result[base] + jump
        if n == 0:
            surface = surface + (0.5 * mask * flux_of[0] + decay[0] * heat)
            sst = surface
        else:
            surface = surface + 0.3 * mask * flux_of[2]
        result[base] = surface
        result[base + 1] = result[base + 1] - jump

    sst_bf = jnp.concatenate([sst, jnp.zeros_like(sst)], 0).astype(BF16)
    column = lax.broadcasted_iota(jnp.int32, (lon_count, 128), 1)
    owner = lax.broadcasted_iota(jnp.int32, (lon_count, 128), 0)
    order = jnp.zeros((lon_count, 128), F32)
    for r in range(ocean_rows):
        for k in range(4):
            p = 4 * r + k
            back = contract(sst_bf, weight[p], 1, 1)
            terms[p : p + 1, :] = back[r : r + 1]
            source = lax.rem(lax.shift_right_logical(index_ref[r, 0, k], 6), lon_count)
            order = jnp.where((column == p) & (owner == source), 1.0, order)
    terms[pairs:, :] = jnp.zeros((128 - pairs, cells), F32)
    ordered = dot(order.astype(BF16), terms[...].astype(BF16))
    temp_out[:, 0, :] = ordered[:, :128]
    temp_out[:, 1, :] = ordered[:, 128:]
    temp_out[:, 2:, :] = jnp.zeros((lon_count, 6, 128), F32)
    spread_out(temp_out, temp_in, temp_send, temp_recv)

    for k in range(1, levels):
        result[k] = result[k] + decay[k] * heat
    save = pltpu.make_async_copy(result, next_hbm, save_sem)
    save.start()
    for copy in halo_copies:
        copy.wait_send()
    await_bytes(flux_hbm.at[pl.ds(0, lon_count - 1)], flux_send)
    await_bytes(temp_in, temp_recv)
    temp_ref[:, :128] = temp_in[:, 0, :]
    temp_ref[:, 128:] = temp_in[:, 1, :]
    await_bytes(temp_out.at[pl.ds(0, lon_count - 1)], temp_send)
    save.wait()


def depth_fractions(levels):
    k = np.arange(levels, dtype=np.float64)
    return np.exp(-k / 8.0) - np.exp(-(k + 1.0) / 8.0)


def exchange(index, flux, weight, tracers, land_sea):
    sec_count, lon_count = lax.axis_size("sec"), lax.axis_size("lon")
    levels, ocean_rows, cells = tracers.shape[1:]
    pairs = ocean_rows * 4
    lines = 2 * levels * ocean_rows
    padded = -(-(lines + ocean_rows) // 128) * 128
    anywhere = pl.BlockSpec(memory_space=pl.ANY)
    next_flat, temp = pl.pallas_call(
        functools.partial(exchange_kernel, sec_count, lon_count, levels),
        out_shape=(
            jax.ShapeDtypeStruct((2 * levels, ocean_rows, cells), F32),
            jax.ShapeDtypeStruct((lon_count, cells), F32),
        ),
        in_specs=[pl.BlockSpec(memory_space=pltpu.SMEM)] + [anywhere] * 4,
        out_specs=(anywhere, pl.BlockSpec(memory_space=pltpu.VMEM)),
        scratch_shapes=[
            pltpu.VMEM((pairs, cells, cells), BF16),
            pltpu.VMEM((2 * levels, ocean_rows, cells), F32),
            pltpu.VMEM((ocean_rows, cells), jnp.int32),
            pltpu.VMEM((2 * levels, ocean_rows, cells), F32),
            pltpu.VMEM((lon_count, 8, 128), F32),
            pltpu.VMEM((128, cells), F32),
            pltpu.VMEM((lon_count, 8, 128), F32),
            pltpu.VMEM((lon_count, 8, 128), F32),
            pltpu.VMEM((padded, cells), BF16),
            pltpu.VMEM((8, padded), F32),
            pltpu.VMEM((8, padded), F32),
            pltpu.VMEM((8, padded), F32),
            pltpu.VMEM((padded, cells), F32),
            pltpu.VMEM((2 * levels + 16, cells), BF16),
            pltpu.VMEM((2 * levels + 16, cells), BF16),
            pltpu.VMEM((2 * levels + 16, cells), F32),
            pltpu.SemaphoreType.DMA((pairs // 8,)),
            pltpu.SemaphoreType.DMA,
            pltpu.SemaphoreType.DMA,
            pltpu.SemaphoreType.DMA,
            pltpu.SemaphoreType.DMA,
            pltpu.SemaphoreType.DMA,
            pltpu.SemaphoreType.DMA,
            pltpu.SemaphoreType.DMA,
            pltpu.SemaphoreType.DMA((3,)),
            pltpu.SemaphoreType.DMA((3,)),
        ],
        compiler_params=pltpu.CompilerParams(
            vmem_limit_bytes=40 * 2**20, collective_id=0, has_side_effects=True
        ),
        name="coupling_exchange",
    )(
        index,
        flux,
        weight.reshape(pairs, cells, cells),
        tracers.reshape(2 * levels, ocean_rows, cells),
        land_sea,
    )
    return next_flat.reshape(tracers.shape), temp


def per_device(
    atm_state,
    cost_class,
    w_in,
    w_out,
    w_flux,
    feeding_block_index,
    pairwise_remap_weight,
    ocean_tracers,
    land_sea,
):
    column_state_next, flux = physics(cost_class, w_in, w_out, w_flux, atm_state)
    tracer_fields_next, atmos_surface_temp = exchange(
        feeding_block_index, flux, pairwise_remap_weight, ocean_tracers, land_sea
    )
    return (column_state_next, tracer_fields_next, atmos_surface_temp)


def solution(mesh):
    return jax.shard_map(
        per_device,
        mesh=mesh,
        in_specs=(
            P(("sec", "lon", "lat"), None, None),
            P(("sec", "lon", "lat")),
            P(),
            P(),
            P(),
            P("lat", ("sec", "lon"), None),
            P("lat", ("sec", "lon"), None, None, None),
            P(None, None, "lat", ("sec", "lon")),
            P("lat", ("sec", "lon")),
        ),
        out_specs=(
            P(("sec", "lon", "lat"), None, None),
            P(None, None, "lat", ("sec", "lon")),
            P(("sec", "lon", "lat"), None),
        ),
        check_vma=False,
    )
```

```python
import functools

import jax
import jax.numpy as jnp
import numpy as np
from jax import lax
from jax.experimental import pallas as pl
from jax.experimental.pallas import tpu as pltpu
from jax.sharding import PartitionSpec as P

F32 = jnp.float32
BF16 = jnp.bfloat16
MESH = pl.DeviceIdType.MESH


def dot(a, b):
    return jnp.dot(a, b, preferred_element_type=F32)


def contract(a, b, dim_a, dim_b):
    return lax.dot_general(
        a, b, (((dim_a,), (dim_b,)), ((), ())), preferred_element_type=F32
    )


def coupled_kernel(
    sec_count, lon_count, levels, groups, longest,
    cls_ref, index_ref, win_ref, wout_ref, wflux_ref, x_hbm, weight_hbm, tracers_hbm, mask_hbm,
    y_hbm, next_hbm, temp_ref,
    xv, half_in, half_out, mix, flux_out, in_sem, out_sem,
    weight, tracers, land, result, flux_in, terms, temp_out, temp_in,
    rows_bf, edge_out, west_in, east_in, halo, row_out, row_in, row_wide,
    weight_sem, tracer_sem, mask_sem, save_sem,
    flux_send, flux_recv, temp_send, temp_recv, halo_send, halo_recv,
    *state,
):
    sec, lon, lat = lax.axis_index("sec"), lax.axis_index("lon"), lax.axis_index("lat")
    total = sec_count * lon_count
    place = sec * lon_count + lon
    before = lax.rem(place + total - 1, total)
    after = lax.rem(place + 1, total)
    west = (before // lon_count, lax.rem(before, lon_count), lat)
    east = (after // lon_count, lax.rem(after, lon_count), lat)
    across = (sec, lon, 1 - lat)
    ocean_rows, cells = land.shape
    blocks = xv.shape[0]
    zs, ss, hs = state[:blocks], state[blocks : 2 * blocks], state[2 * blocks :]
    width = blocks // groups
    pairs = ocean_rows * 4
    fields = 2 * levels
    lines = fields * ocean_rows

    weight_copies = [
        pltpu.make_async_copy(
            weight_hbm.at[pl.ds(8 * g, 8)], weight.at[pl.ds(8 * g, 8)], weight_sem.at[g]
        )
        for g in range(pairs // 8)
    ]
    tracer_copy = pltpu.make_async_copy(tracers_hbm, tracers, tracer_sem)
    mask_copy = pltpu.make_async_copy(mask_hbm, land, mask_sem)
    def load(g):
        part = pl.ds(g * width, width)
        return pltpu.make_async_copy(x_hbm.at[part], xv.at[part], in_sem.at[g])

    def save(g):
        part = pl.ds(g * width, width)
        return pltpu.make_async_copy(xv.at[part], y_hbm.at[part], out_sem.at[g])

    tracer_copy.start()
    mask_copy.start()
    for g in range(groups):
        load(g).start()
    for copy in weight_copies:
        copy.start()

    barrier = pltpu.get_barrier_semaphore()

    def greet(step, carry):
        peer = lax.rem(lon + step, lon_count)
        pl.semaphore_signal(barrier, inc=1, device_id=(sec, peer, lat), device_id_type=MESH)
        return carry

    for neighbour in (west, east, across):
        pl.semaphore_signal(barrier, inc=1, device_id=neighbour, device_id_type=MESH)
    lax.fori_loop(1, lon_count, greet, 0)

    def spread_out(source, target, send_sem, recv_sem):
        def one(step, carry):
            peer = lax.rem(lon + step, lon_count)
            pltpu.make_async_remote_copy(
                src_ref=source.at[peer],
                dst_ref=target.at[lon],
                send_sem=send_sem,
                recv_sem=recv_sem,
                device_id=(sec, peer, lat),
                device_id_type=MESH,
            ).start()
            return carry

        lax.fori_loop(1, lon_count, one, 0)
        pltpu.make_async_copy(source.at[lon], target.at[lon], recv_sem).start()

    def await_bytes(ref, sem):
        pltpu.make_async_copy(ref, ref, sem).wait()

    tracer_copy.wait()
    mask_copy.wait()
    mask = land[...].astype(F32)
    rows_bf[0:lines, :] = tracers[...].reshape(lines, cells).astype(BF16)
    rows_bf[lines : lines + ocean_rows, :] = mask.astype(BF16)
    rows_bf[lines + ocean_rows :, :] = jnp.zeros(
        (rows_bf.shape[0] - lines - ocean_rows, cells), BF16
    )
    pick_row = lax.broadcasted_iota(jnp.int32, (16, cells), 0)
    pick_lane = lax.broadcasted_iota(jnp.int32, (16, cells), 1)
    pick = jnp.where(
        ((pick_row == 0) & (pick_lane == 0)) | ((pick_row == 1) & (pick_lane == cells - 1)), 1.0, 0.0
    ).astype(BF16)
    edge_out[...] = contract(pick, rows_bf[...], 1, 1)[:8]
    first = tracers[:, 0, :]
    last = tracers[:, ocean_rows - 1, :]
    near = jnp.where(lat == 0, last, first).astype(BF16)
    near_mask = jnp.where(lat == 0, mask[ocean_rows - 1 :], mask[:1])
    row_out[0:fields, :] = near
    row_out[fields:, :] = jnp.broadcast_to(near_mask, (row_out.shape[0] - fields, cells)).astype(
        BF16
    )

    def halo_copy(which, source, target, device):
        return pltpu.make_async_remote_copy(
            src_ref=source,
            dst_ref=target,
            send_sem=halo_send.at[which],
            recv_sem=halo_recv.at[which],
            device_id=device,
            device_id_type=MESH,
        )

    halo_copies = [
        halo_copy(0, edge_out, east_in, west),
        halo_copy(1, edge_out, west_in, east),
        halo_copy(2, row_out, row_in, across),
    ]
    half_in[...] = win_ref[...] * 0.5
    half_out[...] = wout_ref[...] * 0.5
    mix[...] = dot(half_in[...], half_out[...]).astype(BF16)
    for g in range(groups):
        load(g).wait()
        for i in range(g * width, (g + 1) * width):
            z = dot(half_in[...], xv[i])
            zs[i][...] = z
            h = (z + z * jnp.tanh(z)).astype(BF16)
            hs[i][...] = h
            ss[i][...] = h

    def update(counter, carry):
        alive = jnp.full(half_in.shape[:1] + (cells,), jnp.where(cls_ref[0] > counter, 1.0, 0.0)).astype(BF16)
        for i in range(blocks):
            z = zs[i][...] + dot(mix[...], hs[i][...])
            zs[i][...] = z
            h = (z + z * jnp.tanh(z)).astype(BF16)
            hs[i][...] = h
            ss[i][...] = ss[i][...] + h * alive
        return carry

    lax.fori_loop(1, longest, update, 0)
    pl.semaphore_wait(barrier, lon_count + 2)
    for copy in halo_copies:
        copy.start()
    for i in range(blocks):
        xv[i] = (xv[i].astype(F32) + dot(half_out[...], ss[i][...])).astype(BF16)
    for g in range(groups):
        save(g).start()

    batch = 8
    for first in range(0, lon_count, batch):
        slots = [lax.rem(lon + first + i, lon_count) for i in range(batch)]
        for slot in slots:
            flux = dot(wflux_ref[...], xv[slot])
            flux_out[slot, 0:4, :] = flux[:, :128]
            flux_out[slot, 4:8, :] = flux[:, 128:]
        for i, slot in enumerate(slots):
            if first + i == 0:
                pltpu.make_async_copy(flux_out.at[slot], flux_in.at[lon], flux_recv).start()
            else:
                pltpu.make_async_remote_copy(
                    src_ref=flux_out.at[slot],
                    dst_ref=flux_in.at[lon],
                    send_sem=flux_send,
                    recv_sem=flux_recv,
                    device_id=(sec, slot, lat),
                    device_id_type=MESH,
                ).start()

    for copy in halo_copies:
        copy.wait_recv()

    edges = jnp.concatenate([west_in[...], east_in[...]], 0).astype(BF16)
    place_back = jnp.where(
        ((pick_row == 1) & (pick_lane == 0)) | ((pick_row == 8) & (pick_lane == cells - 1)), 1.0, 0.0
    ).astype(BF16)
    halo[...] = contract(edges, place_back, 0, 0)
    row_wide[...] = row_in[...].astype(F32)

    row_at = lax.broadcasted_iota(jnp.int32, (ocean_rows, cells), 0)
    lane_at = lax.broadcasted_iota(jnp.int32, (ocean_rows, cells), 1)
    top, bottom = row_at == 0, row_at == ocean_rows - 1
    left, right = lane_at == 0, lane_at == cells - 1

    def neighbours(value, side, line):
        return (
            jnp.where(left, side, pltpu.roll(value, 1, 1)),
            jnp.where(right, side, pltpu.roll(value, cells - 1, 1)),
            jnp.where(top, line, pltpu.roll(value, 1, 0)),
            jnp.where(bottom, line, pltpu.roll(value, ocean_rows - 1, 0)),
        )

    mask_w, mask_e, mask_n, mask_s = neighbours(
        mask, halo[lines : lines + ocean_rows, :], row_wide[fields : fields + 1, :]
    )
    mask_w = jnp.where(left & (place == 0), 0.0, mask_w) * 0.2
    mask_e = jnp.where(right & (place == total - 1), 0.0, mask_e) * 0.2
    mask_n = jnp.where(top & (lat == 0), 0.0, mask_n) * 0.2
    mask_s = jnp.where(bottom & (lat == 1), 0.0, mask_s) * 0.2
    mask_sum = mask_w + mask_e + mask_n + mask_s

    def sideways(field, here):
        w, e, n, s = neighbours(
            here,
            halo[pl.ds(pl.multiple_of(field * ocean_rows, ocean_rows), ocean_rows), :],
            row_wide[pl.ds(field, 1), :],
        )
        return mask_w * w + mask_e * e + mask_n * n + mask_s * s - mask_sum * here

    surface = [tracers[0], tracers[levels]]
    calm = [
        here + mask * sideways(field, here)
        for field, here in zip((0, levels), surface)
    ]

    await_bytes(flux_in, flux_recv)
    for copy in weight_copies:
        copy.wait()
    forcing = []
    for r in range(ocean_rows):
        total_flux = None
        for k in range(4):
            source = lax.rem(lax.shift_right_logical(index_ref[k, r], 6), lon_count)
            tile = flux_in[source]
            lhs = jnp.concatenate([tile[0:4], tile[4:8]], 1).astype(BF16)
            part = dot(lhs, weight[4 * r + k])
            total_flux = part if total_flux is None else total_flux + part
        forcing.append(total_flux)
    flux_of = [
        jnp.concatenate([forcing[r][f : f + 1] for r in range(ocean_rows)], 0) for f in range(4)
    ]

    square = flux_of[3] * flux_of[3]
    top_mixing = mask * (0.1 + 0.3 * square / (1.0 + square))
    ratio = float(np.exp(-1.0 / 8.0))
    heat = (0.5 * (1.0 - ratio)) * (mask * flux_of[1])
    second = [tracers[1], tracers[levels + 1]]
    descent = [top_mixing * (b - a) for a, b in zip(surface, second)]
    sst = calm[0] + descent[0] + (0.5 * mask * flux_of[0] + heat)
    result[0] = sst
    result[levels] = calm[1] + descent[1] + 0.3 * mask * flux_of[2]

    sst_bf = jnp.concatenate([sst, jnp.zeros_like(sst)], 0).astype(BF16)
    column = lax.broadcasted_iota(jnp.int32, (lon_count, 128), 1)
    owner = lax.broadcasted_iota(jnp.int32, (lon_count, 128), 0)
    order = jnp.zeros((lon_count, 128), F32)
    for r in range(ocean_rows):
        for k in range(4):
            p = 4 * r + k
            back = contract(sst_bf, weight[p], 1, 1)
            terms[p : p + 1, :] = back[r : r + 1]
            source = lax.rem(lax.shift_right_logical(index_ref[k, r], 6), lon_count)
            order = jnp.where((column == p) & (owner == source), 1.0, order)
    terms[pairs:, :] = jnp.zeros((128 - pairs, cells), F32)
    ordered = dot(order.astype(BF16), terms[...].astype(BF16))
    temp_out[:, 0, :] = ordered[:, :128]
    temp_out[:, 1, :] = ordered[:, 128:]
    spread_out(temp_out, temp_in, temp_send, temp_recv)

    mixing = 0.1 * mask

    def deeper(k, carry):
        warm, warm_flux, salt, salt_flux, heat = carry
        lower = jnp.minimum(k + 1, levels - 1)
        heat = heat * ratio
        out = []
        for n, here, above in ((0, warm, warm_flux), (1, salt, salt_flux)):
            base = n * levels
            below = tracers[base + lower]
            flux = mixing * (below - here)
            new = here + mask * sideways(base + k, here) + (flux - above)
            result[base + k] = new + heat if n == 0 else new
            out += [below, flux]
        return (*out, heat)

    lax.fori_loop(
        1, levels, deeper, (second[0], descent[0], second[1], descent[1], heat), unroll=3
    )
    save_next = pltpu.make_async_copy(result, next_hbm, save_sem)
    save_next.start()
    for copy in halo_copies:
        copy.wait_send()
    await_bytes(flux_out.at[pl.ds(0, lon_count - 1)], flux_send)
    await_bytes(temp_in, temp_recv)
    temp_ref[:, :128] = temp_in[:, 0, :]
    temp_ref[:, 128:] = temp_in[:, 1, :]
    await_bytes(temp_out.at[pl.ds(0, lon_count - 1)], temp_send)
    save_next.wait()
    for g in range(groups):
        save(g).wait()


def in_hbm(array):
    return pltpu.with_memory_space_constraint(array, pltpu.HBM)


def coupled(
    cost_class, index, w_in, w_out, w_flux, atm_state, weight, tracers, land_sea
):
    sec_count, lon_count = lax.axis_size("sec"), lax.axis_size("lon")
    levels, ocean_rows, cells = tracers.shape[1:]
    blocks, feat = atm_state.shape[:2]
    hid = w_in.shape[0]
    longest, groups = 8, 4
    pairs = ocean_rows * 4
    fields = 2 * levels
    lines = fields * ocean_rows
    padded = -(-(lines + ocean_rows) // 128) * 128
    anywhere = pl.BlockSpec(memory_space=pl.ANY)
    hbm = pl.BlockSpec(memory_space=pltpu.HBM)
    smem = pl.BlockSpec(memory_space=pltpu.SMEM)
    vmem = pl.BlockSpec(memory_space=pltpu.VMEM)
    state, next_flat, temp = pl.pallas_call(
        functools.partial(coupled_kernel, sec_count, lon_count, levels, groups, longest),
        out_shape=(
            pltpu.VMEM(atm_state.shape, BF16),
            pltpu.VMEM((fields, ocean_rows, cells), F32),
            pltpu.VMEM((lon_count, cells), F32),
        ),
        in_specs=[smem, smem, vmem, vmem, vmem, hbm, hbm, hbm, hbm],
        out_specs=(anywhere, anywhere, vmem),
        scratch_shapes=[
            pltpu.VMEM((blocks, feat, cells), BF16),
            pltpu.VMEM((hid, feat), BF16),
            pltpu.VMEM((feat, hid), BF16),
            pltpu.VMEM((hid, hid), BF16),
            pltpu.VMEM((lon_count, 8, 128), F32),
            pltpu.SemaphoreType.DMA((groups,)),
            pltpu.SemaphoreType.DMA((groups,)),
            pltpu.VMEM((pairs, cells, cells), BF16),
            pltpu.VMEM((fields, ocean_rows, cells), F32),
            pltpu.VMEM((ocean_rows, cells), jnp.int32),
            pltpu.VMEM((fields, ocean_rows, cells), F32),
            pltpu.VMEM((lon_count, 8, 128), F32),
            pltpu.VMEM((128, cells), F32),
            pltpu.VMEM((lon_count, 2, 128), F32),
            pltpu.VMEM((lon_count, 2, 128), F32),
            pltpu.VMEM((padded, cells), BF16),
            pltpu.VMEM((8, padded), F32),
            pltpu.VMEM((8, padded), F32),
            pltpu.VMEM((8, padded), F32),
            pltpu.VMEM((padded, cells), F32),
            pltpu.VMEM((fields + 16, cells), BF16),
            pltpu.VMEM((fields + 16, cells), BF16),
            pltpu.VMEM((fields + 16, cells), F32),
            pltpu.SemaphoreType.DMA((pairs // 8,)),
            pltpu.SemaphoreType.DMA,
            pltpu.SemaphoreType.DMA,
            pltpu.SemaphoreType.DMA,
            pltpu.SemaphoreType.DMA,
            pltpu.SemaphoreType.DMA,
            pltpu.SemaphoreType.DMA,
            pltpu.SemaphoreType.DMA,
            pltpu.SemaphoreType.DMA((3,)),
            pltpu.SemaphoreType.DMA((3,)),
        ]
        + [pltpu.VMEM((hid, cells), F32)] * blocks
        + [pltpu.VMEM((hid, cells), BF16)] * (2 * blocks),
        compiler_params=pltpu.CompilerParams(
            vmem_limit_bytes=50 * 2**20, collective_id=0, has_side_effects=True
        ),
        name="coupled_step",
    )(
        cost_class,
        index[:, 0].T,
        w_in,
        w_out,
        w_flux,
        in_hbm(atm_state),
        in_hbm(weight.reshape(pairs, cells, cells)),
        in_hbm(tracers.reshape(fields, ocean_rows, cells)),
        in_hbm(land_sea),
    )
    return state, next_flat.reshape(tracers.shape), temp


def per_device(
    atm_state,
    cost_class,
    w_in,
    w_out,
    w_flux,
    feeding_block_index,
    pairwise_remap_weight,
    ocean_tracers,
    land_sea,
):
    return coupled(
        cost_class,
        feeding_block_index,
        w_in,
        w_out,
        w_flux,
        atm_state,
        pairwise_remap_weight,
        ocean_tracers,
        land_sea,
    )


def solution(mesh):
    return jax.shard_map(
        per_device,
        mesh=mesh,
        in_specs=(
            P(("sec", "lon", "lat"), None, None),
            P(("sec", "lon", "lat")),
            P(),
            P(),
            P(),
            P("lat", ("sec", "lon"), None),
            P("lat", ("sec", "lon"), None, None, None),
            P(None, None, "lat", ("sec", "lon")),
            P("lat", ("sec", "lon")),
        ),
        out_specs=(
            P(("sec", "lon", "lat"), None, None),
            P(None, None, "lat", ("sec", "lon")),
            P(("sec", "lon", "lat"), None),
        ),
        check_vma=False,
    )
```

```python
import functools

import jax
import jax.numpy as jnp
import numpy as np
from jax import lax
from jax.experimental import pallas as pl
from jax.experimental.pallas import tpu as pltpu
from jax.sharding import PartitionSpec as P

F32 = jnp.float32
BF16 = jnp.bfloat16
MESH = pl.DeviceIdType.MESH


def dot(a, b):
    return jnp.dot(a, b, preferred_element_type=F32)


def contract(a, b, dim_a, dim_b):
    return lax.dot_general(
        a, b, (((dim_a,), (dim_b,)), ((), ())), preferred_element_type=F32
    )


def coupled_kernel(
    sec_count, lon_count, levels, groups, longest,
    cls_ref, index_ref, win_ref, wout_ref, wflux_ref, x_hbm, weight_hbm, tracers_hbm, mask_hbm,
    y_hbm, next_hbm, temp_in,
    xv, half_in, half_out, mix, flux_mix, flux_out, in_sem, out_sem, w_sem,
    weight, tracers, land, result, flux_in, terms, temp_out,
    rows_bf, edge_out, west_in, east_in, halo, row_out, row_in, row_wide,
    weight_sem, tracer_sem, mask_sem, save_sem,
    flux_send, flux_recv, temp_send, temp_recv, halo_send, halo_recv,
    *state,
):
    sec, lon, lat = lax.axis_index("sec"), lax.axis_index("lon"), lax.axis_index("lat")
    total = sec_count * lon_count
    place = sec * lon_count + lon
    before = lax.rem(place + total - 1, total)
    after = lax.rem(place + 1, total)
    west = (before // lon_count, lax.rem(before, lon_count), lat)
    east = (after // lon_count, lax.rem(after, lon_count), lat)
    across = (sec, lon, 1 - lat)
    ocean_rows, cells = land.shape
    blocks = xv.shape[0]
    zs, ss, hs = state[:blocks], state[blocks : 2 * blocks], state[2 * blocks :]
    width = blocks // groups
    pairs = ocean_rows * 4
    fields = 2 * levels
    lines = fields * ocean_rows

    weight_copies = [
        pltpu.make_async_copy(
            weight_hbm.at[pl.ds(8 * g, 8)], weight.at[pl.ds(8 * g, 8)], weight_sem.at[g]
        )
        for g in range(pairs // 8)
    ]
    tracer_copy = pltpu.make_async_copy(tracers_hbm, tracers, tracer_sem)
    mask_copy = pltpu.make_async_copy(mask_hbm, land, mask_sem)
    def load(g):
        part = pl.ds(g * width, width)
        return pltpu.make_async_copy(x_hbm.at[part], xv.at[part], in_sem.at[g])

    def save(g):
        part = pl.ds(g * width, width)
        return pltpu.make_async_copy(xv.at[part], y_hbm.at[part], out_sem.at[g])

    hid = wout_ref.shape[1]
    w_in_copy = pltpu.make_async_copy(win_ref, half_in.at[pl.ds(0, hid)], w_sem.at[0])
    w_out_copy = pltpu.make_async_copy(wout_ref, half_out, w_sem.at[1])
    w_in_copy.start()
    w_out_copy.start()
    tracer_copy.start()
    mask_copy.start()
    for g in range(groups):
        load(g).start()

    barrier = pltpu.get_barrier_semaphore()

    def greet(step, carry):
        peer = lax.rem(lon + step, lon_count)
        pl.semaphore_signal(barrier, inc=1, device_id=(sec, peer, lat), device_id_type=MESH)
        return carry

    for neighbour in (west, east, across):
        pl.semaphore_signal(barrier, inc=1, device_id=neighbour, device_id_type=MESH)
    lax.fori_loop(1, lon_count, greet, 0)

    line = 4
    plane = line * line
    at_z, at_y, at_x = lon // plane, lax.rem(lon // line, line), lax.rem(lon, line)

    def hops(step):
        dy, dx = step // line % line, step % line
        return step // plane + min(dy, line - dy) + min(dx, line - dx)

    peers = [
        lax.rem(at_z + step // plane, lon_count // plane) * plane
        + lax.rem(at_y + step // line, line) * line
        + lax.rem(at_x + step, line)
        for step in sorted(range(1, lon_count), key=hops, reverse=True)
    ]

    def spread_out(source, target, send_sem, recv_sem):
        for peer in peers:
            pltpu.make_async_remote_copy(
                src_ref=source.at[peer],
                dst_ref=target.at[lon],
                send_sem=send_sem,
                recv_sem=recv_sem,
                device_id=(sec, peer, lat),
                device_id_type=MESH,
            ).start()
        pltpu.make_async_copy(source.at[lon], target.at[lon], recv_sem).start()

    def await_bytes(ref, sem):
        pltpu.make_async_copy(ref, ref, sem).wait()

    tracer_copy.wait()
    mask_copy.wait()
    mask = land[...].astype(F32)
    rows_bf[0:lines, :] = tracers[...].reshape(lines, cells).astype(BF16)
    rows_bf[lines : lines + ocean_rows, :] = mask.astype(BF16)
    rows_bf[lines + ocean_rows :, :] = jnp.zeros(
        (rows_bf.shape[0] - lines - ocean_rows, cells), BF16
    )
    pick_row = lax.broadcasted_iota(jnp.int32, (16, cells), 0)
    pick_lane = lax.broadcasted_iota(jnp.int32, (16, cells), 1)
    pick = jnp.where(
        ((pick_row == 0) & (pick_lane == 0)) | ((pick_row == 1) & (pick_lane == cells - 1)), 1.0, 0.0
    ).astype(BF16)
    edge_out[...] = contract(pick, rows_bf[...], 1, 1)[:8]
    first = tracers[:, 0, :]
    last = tracers[:, ocean_rows - 1, :]
    near = jnp.where(lat == 0, last, first).astype(BF16)
    near_mask = jnp.where(lat == 0, mask[ocean_rows - 1 :], mask[:1])
    row_out[0:fields, :] = near
    row_out[fields:, :] = jnp.broadcast_to(near_mask, (row_out.shape[0] - fields, cells)).astype(
        BF16
    )

    def halo_copy(which, source, target, device):
        return pltpu.make_async_remote_copy(
            src_ref=source,
            dst_ref=target,
            send_sem=halo_send.at[which],
            recv_sem=halo_recv.at[which],
            device_id=device,
            device_id_type=MESH,
        )

    halo_copies = [
        halo_copy(0, edge_out, east_in, west),
        halo_copy(1, edge_out, west_in, east),
        halo_copy(2, row_out, row_in, across),
    ]
    flux_rows = wflux_ref[...].astype(F32)
    flux_rows = jnp.concatenate([flux_rows, jnp.zeros((12, flux_rows.shape[1]), F32)], 0).astype(BF16)
    w_in_copy.wait()
    half_in[0:hid, :] = half_in[0:hid, :] * 0.5
    half_in[hid:, :] = flux_rows
    w_out_copy.wait()
    half_out[...] = half_out[...] * 0.5
    mix[...] = dot(half_in[0:hid, :], half_out[...]).astype(BF16)
    flux_mix[...] = dot(flux_rows, half_out[...]).astype(BF16)
    for g in range(groups):
        load(g).wait()
        for i in range(g * width, (g + 1) * width):
            both = dot(half_in[...], xv[i])
            z = both[:hid]
            flux_out[i, 0:4, :] = both[hid : hid + 4, :128]
            flux_out[i, 4:8, :] = both[hid : hid + 4, 128:]
            zs[i][...] = z
            h = (z + z * jnp.tanh(z)).astype(BF16)
            hs[i][...] = h
            ss[i][...] = h

    for copy in weight_copies:
        copy.start()

    def update(counter, carry):
        alive = jnp.full((hid, cells), jnp.where(cls_ref[0] > counter, 1.0, 0.0)).astype(BF16)
        for i in range(blocks):
            z = zs[i][...] + dot(mix[...], hs[i][...])
            zs[i][...] = z
            h = (z + z * jnp.tanh(z)).astype(BF16)
            hs[i][...] = h
            ss[i][...] = ss[i][...] + h * alive
        return carry

    lax.fori_loop(1, longest, update, 0)
    pl.semaphore_wait(barrier, lon_count + 2)
    for copy in halo_copies:
        copy.start()
    for i in range(blocks):
        flux = dot(flux_mix[...], ss[i][...])
        flux_out[i, 0:4, :] = flux_out[i, 0:4, :] + flux[:4, :128]
        flux_out[i, 4:8, :] = flux_out[i, 4:8, :] + flux[:4, 128:]
    spread_out(flux_out, flux_in, flux_send, flux_recv)

    for i in range(blocks):
        xv[i] = (xv[i].astype(F32) + dot(half_out[...], ss[i][...])).astype(BF16)
    for g in range(groups):
        save(g).start()

    for copy in halo_copies:
        copy.wait_recv()

    edges = jnp.concatenate([west_in[...], east_in[...]], 0).astype(BF16)
    place_back = jnp.where(
        ((pick_row == 1) & (pick_lane == 0)) | ((pick_row == 8) & (pick_lane == cells - 1)), 1.0, 0.0
    ).astype(BF16)
    halo[...] = contract(edges, place_back, 0, 0)
    row_wide[...] = row_in[...].astype(F32)

    row_at = lax.broadcasted_iota(jnp.int32, (ocean_rows, cells), 0)
    lane_at = lax.broadcasted_iota(jnp.int32, (ocean_rows, cells), 1)
    top, bottom = row_at == 0, row_at == ocean_rows - 1
    left, right = lane_at == 0, lane_at == cells - 1

    def neighbours(value, side, line):
        return (
            jnp.where(left, side, pltpu.roll(value, 1, 1)),
            jnp.where(right, side, pltpu.roll(value, cells - 1, 1)),
            jnp.where(top, line, pltpu.roll(value, 1, 0)),
            jnp.where(bottom, line, pltpu.roll(value, ocean_rows - 1, 0)),
        )

    mask_w, mask_e, mask_n, mask_s = neighbours(
        mask, halo[lines : lines + ocean_rows, :], row_wide[fields : fields + 1, :]
    )
    mask_w = jnp.where(left & (place == 0), 0.0, mask_w) * 0.2
    mask_e = jnp.where(right & (place == total - 1), 0.0, mask_e) * 0.2
    mask_n = jnp.where(top & (lat == 0), 0.0, mask_n) * 0.2
    mask_s = jnp.where(bottom & (lat == 1), 0.0, mask_s) * 0.2
    mask_sum = mask_w + mask_e + mask_n + mask_s

    def sideways(field, here):
        w, e, n, s = neighbours(
            here,
            halo[pl.ds(pl.multiple_of(field * ocean_rows, ocean_rows), ocean_rows), :],
            row_wide[pl.ds(field, 1), :],
        )
        return mask_w * w + mask_e * e + mask_n * n + mask_s * s - mask_sum * here

    surface = [tracers[0], tracers[levels]]
    calm = [
        here + mask * sideways(field, here)
        for field, here in zip((0, levels), surface)
    ]

    await_bytes(flux_in, flux_recv)
    for copy in weight_copies:
        copy.wait()
    forcing = []
    for r in range(ocean_rows):
        total_flux = None
        for k in range(4):
            source = lax.rem(lax.shift_right_logical(index_ref[k, r], 6), lon_count)
            tile = flux_in[source]
            lhs = jnp.concatenate([tile[0:4], tile[4:8]], 1).astype(BF16)
            part = dot(lhs, weight[4 * r + k])
            total_flux = part if total_flux is None else total_flux + part
        forcing.append(total_flux)
    flux_of = [
        jnp.concatenate([forcing[r][f : f + 1] for r in range(ocean_rows)], 0) for f in range(4)
    ]

    square = flux_of[3] * flux_of[3]
    top_mixing = mask * (0.1 + 0.3 * square / (1.0 + square))
    ratio = float(np.exp(-1.0 / 8.0))
    heat = (0.5 * (1.0 - ratio)) * (mask * flux_of[1])
    second = [tracers[1], tracers[levels + 1]]
    descent = [top_mixing * (b - a) for a, b in zip(surface, second)]
    sst = calm[0] + descent[0] + (0.5 * mask * flux_of[0] + heat)
    result[0] = sst
    result[levels] = calm[1] + descent[1] + 0.3 * mask * flux_of[2]

    sst_bf = jnp.concatenate([sst, jnp.zeros_like(sst)], 0).astype(BF16)
    column = lax.broadcasted_iota(jnp.int32, (lon_count, 128), 1)
    owner = lax.broadcasted_iota(jnp.int32, (lon_count, 128), 0)
    order = jnp.zeros((lon_count, 128), F32)
    for r in range(ocean_rows):
        for k in range(4):
            p = 4 * r + k
            back = contract(sst_bf, weight[p], 1, 1)
            terms[p : p + 1, :] = back[r : r + 1]
            source = lax.rem(lax.shift_right_logical(index_ref[k, r], 6), lon_count)
            order = jnp.where((column == p) & (owner == source), 1.0, order)
    terms[pairs:, :] = jnp.zeros((128 - pairs, cells), F32)
    ordered = dot(order.astype(BF16), terms[...].astype(BF16))
    temp_out[:, 0, :] = ordered[:, :128]
    temp_out[:, 1, :] = ordered[:, 128:]
    spread_out(temp_out, temp_in, temp_send, temp_recv)

    mixing = 0.1 * mask

    def deeper(k, carry):
        warm, warm_flux, salt, salt_flux, heat = carry
        lower = jnp.minimum(k + 1, levels - 1)
        heat = heat * ratio
        out = []
        for n, here, above in ((0, warm, warm_flux), (1, salt, salt_flux)):
            base = n * levels
            below = tracers[base + lower]
            flux = mixing * (below - here)
            new = here + mask * sideways(base + k, here) + (flux - above)
            result[base + k] = new + heat if n == 0 else new
            out += [below, flux]
        return (*out, heat)

    lax.fori_loop(
        1, levels, deeper, (second[0], descent[0], second[1], descent[1], heat), unroll=3
    )
    save_next = pltpu.make_async_copy(result, next_hbm, save_sem)
    save_next.start()
    for copy in halo_copies:
        copy.wait_send()
    await_bytes(flux_out.at[pl.ds(0, lon_count - 1)], flux_send)
    await_bytes(temp_in, temp_recv)
    await_bytes(temp_out.at[pl.ds(0, lon_count - 1)], temp_send)
    save_next.wait()
    for g in range(groups):
        save(g).wait()


def in_hbm(array):
    return pltpu.with_memory_space_constraint(array, pltpu.HBM)


def store_kernel(parts, state, following, temp, state_out, following_out, temp_out, rows, sem):
    width = state.shape[0] // parts
    copies = [
        pltpu.make_async_copy(
            state.at[pl.ds(g * width, width)], state_out.at[pl.ds(g * width, width)], sem.at[g]
        )
        for g in range(parts)
    ]
    copies.append(pltpu.make_async_copy(following, following_out, sem.at[parts]))
    for copy in copies:
        copy.start()
    rows[:, :128] = temp[:, 0, :]
    rows[:, 128:] = temp[:, 1, :]
    copies.append(pltpu.make_async_copy(rows, temp_out, sem.at[parts + 1]))
    copies[-1].start()
    for copy in copies:
        copy.wait()


def store(state, following, temp):
    parts = 4
    rows = (temp.shape[0], temp.shape[1] * temp.shape[2])
    anywhere = pl.BlockSpec(memory_space=pl.ANY)
    return pl.pallas_call(
        functools.partial(store_kernel, parts),
        out_shape=(
            pltpu.HBM(state.shape, state.dtype),
            pltpu.HBM(following.shape, following.dtype),
            pltpu.HBM(rows, temp.dtype),
        ),
        in_specs=[anywhere, anywhere, pl.BlockSpec(memory_space=pltpu.VMEM)],
        out_specs=(anywhere,) * 3,
        scratch_shapes=[pltpu.VMEM(rows, temp.dtype), pltpu.SemaphoreType.DMA((parts + 2,))],
        compiler_params=pltpu.CompilerParams(vmem_limit_bytes=2 * 2**20),
        name="store_results",
    )(state, following, temp)


def coupled(
    cost_class, index, w_in, w_out, w_flux, atm_state, weight, tracers, land_sea
):
    sec_count, lon_count = lax.axis_size("sec"), lax.axis_size("lon")
    levels, ocean_rows, cells = tracers.shape[1:]
    blocks, feat = atm_state.shape[:2]
    hid = w_in.shape[0]
    longest, groups = 8, 4
    pairs = ocean_rows * 4
    fields = 2 * levels
    lines = fields * ocean_rows
    padded = -(-(lines + ocean_rows) // 128) * 128
    anywhere = pl.BlockSpec(memory_space=pl.ANY)
    hbm = pl.BlockSpec(memory_space=pltpu.HBM)
    smem = pl.BlockSpec(memory_space=pltpu.SMEM)
    vmem = pl.BlockSpec(memory_space=pltpu.VMEM)
    state, next_flat, temp = pl.pallas_call(
        functools.partial(coupled_kernel, sec_count, lon_count, levels, groups, longest),
        out_shape=(
            pltpu.VMEM(atm_state.shape, BF16),
            pltpu.VMEM((fields, ocean_rows, cells), F32),
            pltpu.VMEM((lon_count, 2, 128), F32),
        ),
        in_specs=[smem, smem, hbm, hbm, vmem, hbm, hbm, hbm, hbm],
        out_specs=(anywhere, anywhere, anywhere),
        scratch_shapes=[
            pltpu.VMEM((blocks, feat, cells), BF16),
            pltpu.VMEM((hid + 16, feat), BF16),
            pltpu.VMEM((feat, hid), BF16),
            pltpu.VMEM((hid, hid), BF16),
            pltpu.VMEM((16, hid), BF16),
            pltpu.VMEM((lon_count, 8, 128), F32),
            pltpu.SemaphoreType.DMA((groups,)),
            pltpu.SemaphoreType.DMA((groups,)),
            pltpu.SemaphoreType.DMA((2,)),
            pltpu.VMEM((pairs, cells, cells), BF16),
            pltpu.VMEM((fields, ocean_rows, cells), F32),
            pltpu.VMEM((ocean_rows, cells), jnp.int32),
            pltpu.VMEM((fields, ocean_rows, cells), F32),
            pltpu.VMEM((lon_count, 8, 128), F32),
            pltpu.VMEM((128, cells), F32),
            pltpu.VMEM((lon_count, 2, 128), F32),
            pltpu.VMEM((padded, cells), BF16),
            pltpu.VMEM((8, padded), F32),
            pltpu.VMEM((8, padded), F32),
            pltpu.VMEM((8, padded), F32),
            pltpu.VMEM((padded, cells), F32),
            pltpu.VMEM((fields + 16, cells), BF16),
            pltpu.VMEM((fields + 16, cells), BF16),
            pltpu.VMEM((fields + 16, cells), F32),
            pltpu.SemaphoreType.DMA((pairs // 8,)),
            pltpu.SemaphoreType.DMA,
            pltpu.SemaphoreType.DMA,
            pltpu.SemaphoreType.DMA,
            pltpu.SemaphoreType.DMA,
            pltpu.SemaphoreType.DMA,
            pltpu.SemaphoreType.DMA,
            pltpu.SemaphoreType.DMA,
            pltpu.SemaphoreType.DMA((3,)),
            pltpu.SemaphoreType.DMA((3,)),
        ]
        + [pltpu.VMEM((hid, cells), F32)] * blocks
        + [pltpu.VMEM((hid, cells), BF16)] * (2 * blocks),
        compiler_params=pltpu.CompilerParams(
            vmem_limit_bytes=50 * 2**20, collective_id=0, has_side_effects=True
        ),
        name="coupled_step",
    )(
        cost_class,
        index[:, 0].T,
        in_hbm(w_in),
        in_hbm(w_out),
        w_flux,
        in_hbm(atm_state),
        in_hbm(weight.reshape(pairs, cells, cells)),
        in_hbm(tracers.reshape(fields, ocean_rows, cells)),
        in_hbm(land_sea),
    )
    state, next_flat, temp = store(state, next_flat, temp)
    return state, next_flat.reshape(tracers.shape), temp


def per_device(
    atm_state,
    cost_class,
    w_in,
    w_out,
    w_flux,
    feeding_block_index,
    pairwise_remap_weight,
    ocean_tracers,
    land_sea,
):
    return coupled(
        cost_class,
        feeding_block_index,
        w_in,
        w_out,
        w_flux,
        atm_state,
        pairwise_remap_weight,
        ocean_tracers,
        land_sea,
    )


def solution(mesh):
    return jax.shard_map(
        per_device,
        mesh=mesh,
        in_specs=(
            P(("sec", "lon", "lat"), None, None),
            P(("sec", "lon", "lat")),
            P(),
            P(),
            P(),
            P("lat", ("sec", "lon"), None),
            P("lat", ("sec", "lon"), None, None, None),
            P(None, None, "lat", ("sec", "lon")),
            P("lat", ("sec", "lon")),
        ),
        out_specs=(
            P(("sec", "lon", "lat"), None, None),
            P(None, None, "lat", ("sec", "lon")),
            P(("sec", "lon", "lat"), None),
        ),
        check_vma=False,
    )
```

```python
import functools

import jax
import jax.numpy as jnp
import numpy as np
from jax import lax
from jax.experimental import pallas as pl
from jax.experimental.pallas import tpu as pltpu
from jax.sharding import PartitionSpec as P

F32 = jnp.float32
BF16 = jnp.bfloat16
MESH = pl.DeviceIdType.MESH


def dot(a, b):
    return jnp.dot(a, b, preferred_element_type=F32)


def contract(a, b, dim_a, dim_b):
    return lax.dot_general(
        a, b, (((dim_a,), (dim_b,)), ((), ())), preferred_element_type=F32
    )


def coupled_kernel(
    sec_count, lon_count, levels, groups, longest,
    cls_ref, index_ref, win_ref, wout_ref, wflux_ref, x_hbm, weight_hbm, tracers_hbm, mask_hbm,
    y_hbm, next_hbm, temp_in,
    xv, half_in, half_out, mix, flux_mix, flux_out, in_sem, out_sem, w_sem,
    weight, tracers, land, result, flux_in, terms, temp_out,
    rows_bf, edge_out, west_in, east_in, halo, row_out, row_in, row_wide,
    weight_sem, tracer_sem, mask_sem, save_sem,
    flux_send, flux_recv, temp_send, temp_recv, halo_send, halo_recv,
    *state,
):
    sec, lon, lat = lax.axis_index("sec"), lax.axis_index("lon"), lax.axis_index("lat")
    total = sec_count * lon_count
    place = sec * lon_count + lon
    before = lax.rem(place + total - 1, total)
    after = lax.rem(place + 1, total)
    west = (before // lon_count, lax.rem(before, lon_count), lat)
    east = (after // lon_count, lax.rem(after, lon_count), lat)
    across = (sec, lon, 1 - lat)
    ocean_rows, cells = land.shape
    blocks = xv.shape[0]
    zs, ss, hs = state[:blocks], state[blocks : 2 * blocks], state[2 * blocks :]
    width = blocks // groups
    pairs = ocean_rows * 4
    fields = 2 * levels
    lines = fields * ocean_rows

    weight_copies = [
        pltpu.make_async_copy(
            weight_hbm.at[pl.ds(8 * g, 8)], weight.at[pl.ds(8 * g, 8)], weight_sem.at[g]
        )
        for g in range(pairs // 8)
    ]
    tracer_copy = pltpu.make_async_copy(tracers_hbm, tracers, tracer_sem)
    mask_copy = pltpu.make_async_copy(mask_hbm, land, mask_sem)
    def load(g):
        part = pl.ds(g * width, width)
        return pltpu.make_async_copy(x_hbm.at[part], xv.at[part], in_sem.at[g])

    def save(g):
        part = pl.ds(g * width, width)
        return pltpu.make_async_copy(xv.at[part], y_hbm.at[part], out_sem.at[g])

    hid = wout_ref.shape[1]
    w_in_copy = pltpu.make_async_copy(win_ref, half_in.at[pl.ds(0, hid)], w_sem.at[0])
    w_out_copy = pltpu.make_async_copy(wout_ref, half_out, w_sem.at[1])
    w_in_copy.start()
    w_out_copy.start()
    tracer_copy.start()
    mask_copy.start()
    for g in range(groups):
        load(g).start()

    barrier = pltpu.get_barrier_semaphore()

    def greet(step, carry):
        peer = lax.rem(lon + step, lon_count)
        pl.semaphore_signal(barrier, inc=1, device_id=(sec, peer, lat), device_id_type=MESH)
        return carry

    for neighbour in (west, east, across):
        pl.semaphore_signal(barrier, inc=1, device_id=neighbour, device_id_type=MESH)
    lax.fori_loop(1, lon_count, greet, 0)

    line = 4
    plane = line * line
    at_z, at_y, at_x = lon // plane, lax.rem(lon // line, line), lax.rem(lon, line)

    def hops(step):
        dy, dx = step // line % line, step % line
        return step // plane + min(dy, line - dy) + min(dx, line - dx)

    peers = [
        lax.rem(at_z + step // plane, lon_count // plane) * plane
        + lax.rem(at_y + step // line, line) * line
        + lax.rem(at_x + step, line)
        for step in sorted(range(1, lon_count), key=hops, reverse=True)
    ]

    def spread_out(source, target, send_sem, recv_sem):
        for peer in peers:
            pltpu.make_async_remote_copy(
                src_ref=source.at[peer],
                dst_ref=target.at[lon],
                send_sem=send_sem,
                recv_sem=recv_sem,
                device_id=(sec, peer, lat),
                device_id_type=MESH,
            ).start()
        pltpu.make_async_copy(source.at[lon], target.at[lon], recv_sem).start()

    def await_bytes(ref, sem):
        pltpu.make_async_copy(ref, ref, sem).wait()

    tracer_copy.wait()
    mask_copy.wait()
    mask = land[...].astype(F32)
    rows_bf[0:lines, :] = tracers[...].reshape(lines, cells).astype(BF16)
    rows_bf[lines : lines + ocean_rows, :] = mask.astype(BF16)
    rows_bf[lines + ocean_rows :, :] = jnp.zeros(
        (rows_bf.shape[0] - lines - ocean_rows, cells), BF16
    )
    pick_row = lax.broadcasted_iota(jnp.int32, (16, cells), 0)
    pick_lane = lax.broadcasted_iota(jnp.int32, (16, cells), 1)
    pick = jnp.where(
        ((pick_row == 0) & (pick_lane == 0)) | ((pick_row == 1) & (pick_lane == cells - 1)), 1.0, 0.0
    ).astype(BF16)
    edge_out[...] = contract(pick, rows_bf[...], 1, 1)[:8]
    first = tracers[:, 0, :]
    last = tracers[:, ocean_rows - 1, :]
    near = jnp.where(lat == 0, last, first).astype(BF16)
    near_mask = jnp.where(lat == 0, mask[ocean_rows - 1 :], mask[:1])
    row_out[0:fields, :] = near
    row_out[fields:, :] = jnp.broadcast_to(near_mask, (row_out.shape[0] - fields, cells)).astype(
        BF16
    )

    def halo_copy(which, source, target, device):
        return pltpu.make_async_remote_copy(
            src_ref=source,
            dst_ref=target,
            send_sem=halo_send.at[which],
            recv_sem=halo_recv.at[which],
            device_id=device,
            device_id_type=MESH,
        )

    halo_copies = [
        halo_copy(0, edge_out, east_in, west),
        halo_copy(1, edge_out, west_in, east),
        halo_copy(2, row_out, row_in, across),
    ]
    flux_rows = wflux_ref[...].astype(F32)
    flux_rows = jnp.concatenate([flux_rows, jnp.zeros((12, flux_rows.shape[1]), F32)], 0).astype(BF16)
    w_in_copy.wait()
    half_in[0:hid, :] = half_in[0:hid, :] * 0.5
    half_in[hid:, :] = flux_rows
    w_out_copy.wait()
    half_out[...] = half_out[...] * 0.5
    mix[...] = dot(half_in[0:hid, :], half_out[...]).astype(BF16)
    flux_mix[...] = dot(flux_rows, half_out[...]).astype(BF16)
    for g in range(groups):
        load(g).wait()
        for i in range(g * width, (g + 1) * width):
            both = dot(half_in[...], xv[i])
            z = both[:hid]
            flux_out[i, 0:4, :] = both[hid : hid + 4, :128]
            flux_out[i, 4:8, :] = both[hid : hid + 4, 128:]
            zs[i][...] = z
            h = (z + z * jnp.tanh(z)).astype(BF16)
            hs[i][...] = h
            ss[i][...] = h

    for copy in weight_copies:
        copy.start()

    def update(counter, carry):
        alive = jnp.full((hid, cells), jnp.where(cls_ref[0] > counter, 1.0, 0.0)).astype(BF16)
        for i in range(blocks):
            z = zs[i][...] + dot(mix[...], hs[i][...])
            zs[i][...] = z
            h = (z + z * jnp.tanh(z)).astype(BF16)
            hs[i][...] = h
            ss[i][...] = ss[i][...] + h * alive
        return carry

    lax.fori_loop(1, longest, update, 0)
    pl.semaphore_wait(barrier, lon_count + 2)
    for copy in halo_copies:
        copy.start()
    for i in range(blocks):
        flux = dot(flux_mix[...], ss[i][...])
        flux_out[i, 0:4, :] = flux_out[i, 0:4, :] + flux[:4, :128]
        flux_out[i, 4:8, :] = flux_out[i, 4:8, :] + flux[:4, 128:]
    spread_out(flux_out, flux_in, flux_send, flux_recv)

    for i in range(blocks):
        xv[i] = (xv[i].astype(F32) + dot(half_out[...], ss[i][...])).astype(BF16)
    for g in range(groups):
        save(g).start()

    for copy in halo_copies:
        copy.wait_recv()

    edges = jnp.concatenate([west_in[...], east_in[...]], 0).astype(BF16)
    place_back = jnp.where(
        ((pick_row == 1) & (pick_lane == 0)) | ((pick_row == 8) & (pick_lane == cells - 1)), 1.0, 0.0
    ).astype(BF16)
    halo[...] = contract(edges, place_back, 0, 0)
    row_wide[...] = row_in[...].astype(F32)

    row_at = lax.broadcasted_iota(jnp.int32, (ocean_rows, cells), 0)
    lane_at = lax.broadcasted_iota(jnp.int32, (ocean_rows, cells), 1)
    top, bottom = row_at == 0, row_at == ocean_rows - 1
    left, right = lane_at == 0, lane_at == cells - 1

    def neighbours(value, side, line):
        return (
            jnp.where(left, side, pltpu.roll(value, 1, 1)),
            jnp.where(right, side, pltpu.roll(value, cells - 1, 1)),
            jnp.where(top, line, pltpu.roll(value, 1, 0)),
            jnp.where(bottom, line, pltpu.roll(value, ocean_rows - 1, 0)),
        )

    mask_w, mask_e, mask_n, mask_s = neighbours(
        mask, halo[lines : lines + ocean_rows, :], row_wide[fields : fields + 1, :]
    )
    mask_w = jnp.where(left & (place == 0), 0.0, mask_w) * 0.2
    mask_e = jnp.where(right & (place == total - 1), 0.0, mask_e) * 0.2
    mask_n = jnp.where(top & (lat == 0), 0.0, mask_n) * 0.2
    mask_s = jnp.where(bottom & (lat == 1), 0.0, mask_s) * 0.2
    mask_sum = mask_w + mask_e + mask_n + mask_s

    def sideways(field, here):
        w, e, n, s = neighbours(
            here,
            halo[pl.ds(pl.multiple_of(field * ocean_rows, ocean_rows), ocean_rows), :],
            row_wide[pl.ds(field, 1), :],
        )
        return mask_w * w + mask_e * e + mask_n * n + mask_s * s - mask_sum * here

    surface = [tracers[0], tracers[levels]]
    calm = [
        here + mask * sideways(field, here)
        for field, here in zip((0, levels), surface)
    ]

    await_bytes(flux_in, flux_recv)
    for copy in weight_copies:
        copy.wait()
    forcing = []
    for r in range(ocean_rows):
        total_flux = None
        for k in range(4):
            source = lax.rem(lax.shift_right_logical(index_ref[k, r], 6), lon_count)
            tile = flux_in[source]
            lhs = jnp.concatenate([tile[0:4], tile[4:8]], 1).astype(BF16)
            part = dot(lhs, weight[4 * r + k])
            total_flux = part if total_flux is None else total_flux + part
        forcing.append(total_flux)
    flux_of = [
        jnp.concatenate([forcing[r][f : f + 1] for r in range(ocean_rows)], 0) for f in range(4)
    ]

    square = flux_of[3] * flux_of[3]
    top_mixing = mask * (0.1 + 0.3 * square / (1.0 + square))
    ratio = float(np.exp(-1.0 / 8.0))
    heat = (0.5 * (1.0 - ratio)) * (mask * flux_of[1])
    second = [tracers[1], tracers[levels + 1]]
    descent = [top_mixing * (b - a) for a, b in zip(surface, second)]
    sst = calm[0] + descent[0] + (0.5 * mask * flux_of[0] + heat)
    result[0] = sst
    result[levels] = calm[1] + descent[1] + 0.3 * mask * flux_of[2]

    sst_bf = jnp.concatenate([sst, jnp.zeros_like(sst)], 0).astype(BF16)
    column = lax.broadcasted_iota(jnp.int32, (lon_count, 128), 1)
    owner = lax.broadcasted_iota(jnp.int32, (lon_count, 128), 0)
    order = jnp.zeros((lon_count, 128), F32)
    for r in range(ocean_rows):
        for k in range(4):
            p = 4 * r + k
            back = contract(sst_bf, weight[p], 1, 1)
            terms[p : p + 1, :] = back[r : r + 1]
            source = lax.rem(lax.shift_right_logical(index_ref[k, r], 6), lon_count)
            order = jnp.where((column == p) & (owner == source), 1.0, order)
    terms[pairs:, :] = jnp.zeros((128 - pairs, cells), F32)
    ordered = dot(order.astype(BF16), terms[...].astype(BF16))
    temp_out[:, 0, :] = ordered[:, :128]
    temp_out[:, 1, :] = ordered[:, 128:]
    spread_out(temp_out, temp_in, temp_send, temp_recv)

    mixing = 0.1 * mask

    def deeper(k, carry):
        warm, warm_flux, salt, salt_flux, heat = carry
        lower = jnp.minimum(k + 1, levels - 1)
        heat = heat * ratio
        out = []
        for n, here, above in ((0, warm, warm_flux), (1, salt, salt_flux)):
            base = n * levels
            below = tracers[base + lower]
            flux = mixing * (below - here)
            new = here + mask * sideways(base + k, here) + (flux - above)
            result[base + k] = new + heat if n == 0 else new
            out += [below, flux]
        return (*out, heat)

    lax.fori_loop(
        1, levels, deeper, (second[0], descent[0], second[1], descent[1], heat), unroll=3
    )
    save_next = pltpu.make_async_copy(result, next_hbm, save_sem)
    save_next.start()
    for copy in halo_copies:
        copy.wait_send()
    await_bytes(flux_out.at[pl.ds(0, lon_count - 1)], flux_send)
    await_bytes(temp_in, temp_recv)
    await_bytes(temp_out.at[pl.ds(0, lon_count - 1)], temp_send)
    save_next.wait()
    for g in range(groups):
        save(g).wait()


def in_hbm(array):
    return pltpu.with_memory_space_constraint(array, pltpu.HBM)


def store_kernel(parts, state, following, temp, state_out, following_out, temp_out, rows, sem):
    width = state.shape[0] // parts
    copies = [
        pltpu.make_async_copy(
            state.at[pl.ds(g * width, width)], state_out.at[pl.ds(g * width, width)], sem.at[g]
        )
        for g in range(parts)
    ]
    copies.append(pltpu.make_async_copy(following, following_out, sem.at[parts]))
    for copy in copies:
        copy.start()
    rows[:, :128] = temp[:, 0, :]
    rows[:, 128:] = temp[:, 1, :]
    copies.append(pltpu.make_async_copy(rows, temp_out, sem.at[parts + 1]))
    copies[-1].start()
    for copy in copies:
        copy.wait()


def store(state, following, temp):
    parts = 4
    rows = (temp.shape[0], temp.shape[1] * temp.shape[2])
    anywhere = pl.BlockSpec(memory_space=pl.ANY)
    return pl.pallas_call(
        functools.partial(store_kernel, parts),
        out_shape=(
            pltpu.HBM(state.shape, state.dtype),
            pltpu.HBM(following.shape, following.dtype),
            pltpu.HBM(rows, temp.dtype),
        ),
        in_specs=[anywhere, anywhere, pl.BlockSpec(memory_space=pltpu.VMEM)],
        out_specs=(anywhere,) * 3,
        scratch_shapes=[pltpu.VMEM(rows, temp.dtype), pltpu.SemaphoreType.DMA((parts + 2,))],
        compiler_params=pltpu.CompilerParams(vmem_limit_bytes=2 * 2**20),
        name="store_results",
    )(state, following, temp)


def coupled(
    cost_class, index, w_in, w_out, w_flux, atm_state, weight, tracers, land_sea
):
    sec_count, lon_count = lax.axis_size("sec"), lax.axis_size("lon")
    levels, ocean_rows, cells = tracers.shape[1:]
    blocks, feat = atm_state.shape[:2]
    hid = w_in.shape[0]
    longest, groups = 8, 2
    pairs = ocean_rows * 4
    fields = 2 * levels
    lines = fields * ocean_rows
    padded = -(-(lines + ocean_rows) // 128) * 128
    anywhere = pl.BlockSpec(memory_space=pl.ANY)
    hbm = pl.BlockSpec(memory_space=pltpu.HBM)
    smem = pl.BlockSpec(memory_space=pltpu.SMEM)
    vmem = pl.BlockSpec(memory_space=pltpu.VMEM)
    state, next_flat, temp = pl.pallas_call(
        functools.partial(coupled_kernel, sec_count, lon_count, levels, groups, longest),
        out_shape=(
            pltpu.VMEM(atm_state.shape, BF16),
            pltpu.VMEM((fields, ocean_rows, cells), F32),
            pltpu.VMEM((lon_count, 2, 128), F32),
        ),
        in_specs=[smem, smem, hbm, hbm, vmem, hbm, hbm, hbm, hbm],
        out_specs=(anywhere, anywhere, anywhere),
        scratch_shapes=[
            pltpu.VMEM((blocks, feat, cells), BF16),
            pltpu.VMEM((hid + 16, feat), BF16),
            pltpu.VMEM((feat, hid), BF16),
            pltpu.VMEM((hid, hid), BF16),
            pltpu.VMEM((16, hid), BF16),
            pltpu.VMEM((lon_count, 8, 128), F32),
            pltpu.SemaphoreType.DMA((groups,)),
            pltpu.SemaphoreType.DMA((groups,)),
            pltpu.SemaphoreType.DMA((2,)),
            pltpu.VMEM((pairs, cells, cells), BF16),
            pltpu.VMEM((fields, ocean_rows, cells), F32),
            pltpu.VMEM((ocean_rows, cells), jnp.int32),
            pltpu.VMEM((fields, ocean_rows, cells), F32),
            pltpu.VMEM((lon_count, 8, 128), F32),
            pltpu.VMEM((128, cells), F32),
            pltpu.VMEM((lon_count, 2, 128), F32),
            pltpu.VMEM((padded, cells), BF16),
            pltpu.VMEM((8, padded), F32),
            pltpu.VMEM((8, padded), F32),
            pltpu.VMEM((8, padded), F32),
            pltpu.VMEM((padded, cells), F32),
            pltpu.VMEM((fields + 16, cells), BF16),
            pltpu.VMEM((fields + 16, cells), BF16),
            pltpu.VMEM((fields + 16, cells), F32),
            pltpu.SemaphoreType.DMA((pairs // 8,)),
            pltpu.SemaphoreType.DMA,
            pltpu.SemaphoreType.DMA,
            pltpu.SemaphoreType.DMA,
            pltpu.SemaphoreType.DMA,
            pltpu.SemaphoreType.DMA,
            pltpu.SemaphoreType.DMA,
            pltpu.SemaphoreType.DMA,
            pltpu.SemaphoreType.DMA((3,)),
            pltpu.SemaphoreType.DMA((3,)),
        ]
        + [pltpu.VMEM((hid, cells), F32)] * blocks
        + [pltpu.VMEM((hid, cells), BF16)] * (2 * blocks),
        compiler_params=pltpu.CompilerParams(
            vmem_limit_bytes=50 * 2**20, collective_id=0, has_side_effects=True
        ),
        name="coupled_step",
    )(
        cost_class,
        index[:, 0].T,
        in_hbm(w_in),
        in_hbm(w_out),
        w_flux,
        in_hbm(atm_state),
        in_hbm(weight.reshape(pairs, cells, cells)),
        in_hbm(tracers.reshape(fields, ocean_rows, cells)),
        in_hbm(land_sea),
    )
    state, next_flat, temp = store(state, next_flat, temp)
    return state, next_flat.reshape(tracers.shape), temp


def per_device(
    atm_state,
    cost_class,
    w_in,
    w_out,
    w_flux,
    feeding_block_index,
    pairwise_remap_weight,
    ocean_tracers,
    land_sea,
):
    return coupled(
        cost_class,
        feeding_block_index,
        w_in,
        w_out,
        w_flux,
        atm_state,
        pairwise_remap_weight,
        ocean_tracers,
        land_sea,
    )


def solution(mesh):
    return jax.shard_map(
        per_device,
        mesh=mesh,
        in_specs=(
            P(("sec", "lon", "lat"), None, None),
            P(("sec", "lon", "lat")),
            P(),
            P(),
            P(),
            P("lat", ("sec", "lon"), None),
            P("lat", ("sec", "lon"), None, None, None),
            P(None, None, "lat", ("sec", "lon")),
            P("lat", ("sec", "lon")),
        ),
        out_specs=(
            P(("sec", "lon", "lat"), None, None),
            P(None, None, "lat", ("sec", "lon")),
            P(("sec", "lon", "lat"), None),
        ),
        check_vma=False,
    )
```

```python
import functools

import jax
import jax.numpy as jnp
import numpy as np
from jax import lax
from jax.experimental import pallas as pl
from jax.experimental.pallas import tpu as pltpu
from jax.sharding import PartitionSpec as P

F32 = jnp.float32
BF16 = jnp.bfloat16
MESH = pl.DeviceIdType.MESH


def dot(a, b):
    return jnp.dot(a, b, preferred_element_type=F32)


def contract(a, b, dim_a, dim_b):
    return lax.dot_general(
        a, b, (((dim_a,), (dim_b,)), ((), ())), preferred_element_type=F32
    )


def coupled_kernel(
    sec_count, lon_count, levels, groups, longest,
    cls_ref, index_ref, win_ref, wout_ref, wflux_ref, x_hbm, weight_hbm, tracers_hbm, mask_hbm,
    y_hbm, next_hbm, temp_in,
    xv, half_in, half_out, mix, flux_mix, flux_out, in_sem, out_sem, w_sem,
    weight, tracers, land, result, flux_in, terms, temp_out,
    rows_bf, edge_out, west_in, east_in, halo, row_out, row_in, row_wide,
    weight_sem, tracer_sem, mask_sem, save_sem,
    flux_send, flux_recv, temp_send, temp_recv, halo_send, halo_recv,
    *state,
):
    sec, lon, lat = lax.axis_index("sec"), lax.axis_index("lon"), lax.axis_index("lat")
    total = sec_count * lon_count
    place = sec * lon_count + lon
    before = lax.rem(place + total - 1, total)
    after = lax.rem(place + 1, total)
    west = (before // lon_count, lax.rem(before, lon_count), lat)
    east = (after // lon_count, lax.rem(after, lon_count), lat)
    across = (sec, lon, 1 - lat)
    ocean_rows, cells = land.shape
    blocks = xv.shape[0]
    zs, ss, hs = state[:blocks], state[blocks : 2 * blocks], state[2 * blocks :]
    width = blocks // groups
    pairs = ocean_rows * 4
    fields = 2 * levels
    lines = fields * ocean_rows

    weight_copies = [
        pltpu.make_async_copy(
            weight_hbm.at[pl.ds(8 * g, 8)], weight.at[pl.ds(8 * g, 8)], weight_sem.at[g]
        )
        for g in range(pairs // 8)
    ]
    tracer_copy = pltpu.make_async_copy(tracers_hbm, tracers, tracer_sem)
    mask_copy = pltpu.make_async_copy(mask_hbm, land, mask_sem)
    def load(g):
        part = pl.ds(g * width, width)
        return pltpu.make_async_copy(x_hbm.at[part], xv.at[part], in_sem.at[g])

    def save(g):
        part = pl.ds(g * width, width)
        return pltpu.make_async_copy(xv.at[part], y_hbm.at[part], out_sem.at[g])

    hid = wout_ref.shape[1]
    w_in_copy = pltpu.make_async_copy(win_ref, half_in.at[pl.ds(0, hid)], w_sem.at[0])
    w_out_copy = pltpu.make_async_copy(wout_ref, half_out, w_sem.at[1])
    w_in_copy.start()
    w_out_copy.start()
    tracer_copy.start()
    mask_copy.start()
    for g in range(groups):
        load(g).start()

    barrier = pltpu.get_barrier_semaphore()

    def greet(step, carry):
        peer = lax.rem(lon + step, lon_count)
        pl.semaphore_signal(barrier, inc=1, device_id=(sec, peer, lat), device_id_type=MESH)
        return carry

    for neighbour in (west, east, across):
        pl.semaphore_signal(barrier, inc=1, device_id=neighbour, device_id_type=MESH)
    lax.fori_loop(1, lon_count, greet, 0)

    line = 4
    plane = line * line
    at_z, at_y, at_x = lon // plane, lax.rem(lon // line, line), lax.rem(lon, line)

    def hops(step):
        dy, dx = step // line % line, step % line
        return step // plane + min(dy, line - dy) + min(dx, line - dx)

    peers = [
        lax.rem(at_z + step // plane, lon_count // plane) * plane
        + lax.rem(at_y + step // line, line) * line
        + lax.rem(at_x + step, line)
        for step in sorted(range(1, lon_count), key=hops, reverse=True)
    ]

    def spread_out(source, target, send_sem, recv_sem):
        for peer in peers:
            pltpu.make_async_remote_copy(
                src_ref=source.at[peer],
                dst_ref=target.at[lon],
                send_sem=send_sem,
                recv_sem=recv_sem,
                device_id=(sec, peer, lat),
                device_id_type=MESH,
            ).start()
        pltpu.make_async_copy(source.at[lon], target.at[lon], recv_sem).start()

    def await_bytes(ref, sem):
        pltpu.make_async_copy(ref, ref, sem).wait()

    tracer_copy.wait()
    mask_copy.wait()
    mask = land[...].astype(F32)
    rows_bf[0:lines, :] = tracers[...].reshape(lines, cells).astype(BF16)
    rows_bf[lines : lines + ocean_rows, :] = mask.astype(BF16)
    rows_bf[lines + ocean_rows :, :] = jnp.zeros(
        (rows_bf.shape[0] - lines - ocean_rows, cells), BF16
    )
    pick_row = lax.broadcasted_iota(jnp.int32, (16, cells), 0)
    pick_lane = lax.broadcasted_iota(jnp.int32, (16, cells), 1)
    pick = jnp.where(
        ((pick_row == 0) & (pick_lane == 0)) | ((pick_row == 1) & (pick_lane == cells - 1)), 1.0, 0.0
    ).astype(BF16)
    edge_out[...] = contract(pick, rows_bf[...], 1, 1)[:8]
    first = tracers[:, 0, :]
    last = tracers[:, ocean_rows - 1, :]
    near = jnp.where(lat == 0, last, first).astype(BF16)
    near_mask = jnp.where(lat == 0, mask[ocean_rows - 1 :], mask[:1])
    row_out[0:fields, :] = near
    row_out[fields:, :] = jnp.broadcast_to(near_mask, (row_out.shape[0] - fields, cells)).astype(
        BF16
    )

    def halo_copy(which, source, target, device):
        return pltpu.make_async_remote_copy(
            src_ref=source,
            dst_ref=target,
            send_sem=halo_send.at[which],
            recv_sem=halo_recv.at[which],
            device_id=device,
            device_id_type=MESH,
        )

    halo_copies = [
        halo_copy(0, edge_out, east_in, west),
        halo_copy(1, edge_out, west_in, east),
        halo_copy(2, row_out, row_in, across),
    ]
    flux_rows = wflux_ref[...].astype(F32)
    flux_rows = jnp.concatenate([flux_rows, jnp.zeros((12, flux_rows.shape[1]), F32)], 0).astype(BF16)
    w_in_copy.wait()
    half_in[0:hid, :] = half_in[0:hid, :] * 0.5
    half_in[hid:, :] = flux_rows
    w_out_copy.wait()
    half_out[...] = half_out[...] * 0.5
    mix[...] = dot(half_in[0:hid, :], half_out[...]).astype(BF16)
    flux_mix[...] = dot(flux_rows, half_out[...]).astype(BF16)
    for g in range(groups):
        load(g).wait()
        for i in range(g * width, (g + 1) * width):
            both = dot(half_in[...], xv[i])
            z = both[:hid]
            flux_out[i] = both[hid : hid + 4]
            zs[i][...] = z
            h = (z + z * jnp.tanh(z)).astype(BF16)
            hs[i][...] = h
            ss[i][...] = h

    for copy in weight_copies:
        copy.start()

    def update(counter, carry):
        alive = jnp.full((hid, cells), jnp.where(cls_ref[0] > counter, 1.0, 0.0)).astype(BF16)
        for i in range(blocks):
            z = zs[i][...] + dot(mix[...], hs[i][...])
            zs[i][...] = z
            h = (z + z * jnp.tanh(z)).astype(BF16)
            hs[i][...] = h
            ss[i][...] = ss[i][...] + h * alive
        return carry

    lax.fori_loop(1, longest, update, 0)
    pl.semaphore_wait(barrier, lon_count + 2)
    for copy in halo_copies:
        copy.start()
    for i in range(blocks):
        flux = dot(flux_mix[...], ss[i][...])
        flux_out[i] = flux_out[i] + flux[:4]
    spread_out(flux_out, flux_in, flux_send, flux_recv)

    for i in range(blocks):
        xv[i] = (xv[i].astype(F32) + dot(half_out[...], ss[i][...])).astype(BF16)
    for g in range(groups):
        save(g).start()

    for copy in halo_copies:
        copy.wait_recv()

    edges = jnp.concatenate([west_in[...], east_in[...]], 0).astype(BF16)
    place_back = jnp.where(
        ((pick_row == 1) & (pick_lane == 0)) | ((pick_row == 8) & (pick_lane == cells - 1)), 1.0, 0.0
    ).astype(BF16)
    halo[...] = contract(edges, place_back, 0, 0)
    row_wide[...] = row_in[...].astype(F32)

    row_at = lax.broadcasted_iota(jnp.int32, (ocean_rows, cells), 0)
    lane_at = lax.broadcasted_iota(jnp.int32, (ocean_rows, cells), 1)
    top, bottom = row_at == 0, row_at == ocean_rows - 1
    left, right = lane_at == 0, lane_at == cells - 1

    def neighbours(value, side, line):
        return (
            jnp.where(left, side, pltpu.roll(value, 1, 1)),
            jnp.where(right, side, pltpu.roll(value, cells - 1, 1)),
            jnp.where(top, line, pltpu.roll(value, 1, 0)),
            jnp.where(bottom, line, pltpu.roll(value, ocean_rows - 1, 0)),
        )

    mask_w, mask_e, mask_n, mask_s = neighbours(
        mask, halo[lines : lines + ocean_rows, :], row_wide[fields : fields + 1, :]
    )
    mask_w = jnp.where(left & (place == 0), 0.0, mask_w) * 0.2
    mask_e = jnp.where(right & (place == total - 1), 0.0, mask_e) * 0.2
    mask_n = jnp.where(top & (lat == 0), 0.0, mask_n) * 0.2
    mask_s = jnp.where(bottom & (lat == 1), 0.0, mask_s) * 0.2
    mask_sum = mask_w + mask_e + mask_n + mask_s

    def sideways(field, here):
        w, e, n, s = neighbours(
            here,
            halo[pl.ds(pl.multiple_of(field * ocean_rows, ocean_rows), ocean_rows), :],
            row_wide[pl.ds(field, 1), :],
        )
        return mask_w * w + mask_e * e + mask_n * n + mask_s * s - mask_sum * here

    surface = [tracers[0], tracers[levels]]
    calm = [
        here + mask * sideways(field, here)
        for field, here in zip((0, levels), surface)
    ]

    column = lax.broadcasted_iota(jnp.int32, (lon_count, 128), 1)
    owner = lax.broadcasted_iota(jnp.int32, (lon_count, 128), 0)
    order = jnp.zeros((lon_count, 128), F32)
    for r in range(ocean_rows):
        for k in range(4):
            source = lax.rem(lax.shift_right_logical(index_ref[k, r], 6), lon_count)
            order = jnp.where((column == 4 * r + k) & (owner == source), 1.0, order)
    order = order.astype(BF16)
    terms[pairs:, :] = jnp.zeros((128 - pairs, cells), F32)

    await_bytes(flux_in, flux_recv)
    for copy in weight_copies:
        copy.wait()
    forcing = []
    for r in range(ocean_rows):
        total_flux = None
        for k in range(4):
            source = lax.rem(lax.shift_right_logical(index_ref[k, r], 6), lon_count)
            lhs = flux_in[source].astype(BF16)
            part = dot(lhs, weight[4 * r + k])
            total_flux = part if total_flux is None else total_flux + part
        forcing.append(total_flux)
    flux_of = [
        jnp.concatenate([forcing[r][f : f + 1] for r in range(ocean_rows)], 0) for f in range(4)
    ]

    square = flux_of[3] * flux_of[3]
    top_mixing = mask * (0.1 + 0.3 * square / (1.0 + square))
    ratio = float(np.exp(-1.0 / 8.0))
    heat = (0.5 * (1.0 - ratio)) * (mask * flux_of[1])
    second = [tracers[1], tracers[levels + 1]]
    descent = [top_mixing * (b - a) for a, b in zip(surface, second)]
    sst = calm[0] + descent[0] + (0.5 * mask * flux_of[0] + heat)
    result[0] = sst
    result[levels] = calm[1] + descent[1] + 0.3 * mask * flux_of[2]

    sst_bf = jnp.concatenate([sst, jnp.zeros_like(sst)], 0).astype(BF16)
    for r in range(ocean_rows):
        for k in range(4):
            p = 4 * r + k
            back = contract(sst_bf, weight[p], 1, 1)
            terms[p : p + 1, :] = back[r : r + 1]
    ordered = dot(order, terms[...].astype(BF16))
    temp_out[:, 0, :] = ordered[:, :128]
    temp_out[:, 1, :] = ordered[:, 128:]
    spread_out(temp_out, temp_in, temp_send, temp_recv)

    mixing = 0.1 * mask

    def deeper(k, carry):
        warm, warm_flux, salt, salt_flux, heat = carry
        lower = jnp.minimum(k + 1, levels - 1)
        heat = heat * ratio
        out = []
        for n, here, above in ((0, warm, warm_flux), (1, salt, salt_flux)):
            base = n * levels
            below = tracers[base + lower]
            flux = mixing * (below - here)
            new = here + mask * sideways(base + k, here) + (flux - above)
            result[base + k] = new + heat if n == 0 else new
            out += [below, flux]
        return (*out, heat)

    lax.fori_loop(
        1, levels, deeper, (second[0], descent[0], second[1], descent[1], heat), unroll=3
    )
    save_next = pltpu.make_async_copy(result, next_hbm, save_sem)
    save_next.start()
    for copy in halo_copies:
        copy.wait_send()
    await_bytes(flux_out.at[pl.ds(0, lon_count - 1)], flux_send)
    await_bytes(temp_in, temp_recv)
    await_bytes(temp_out.at[pl.ds(0, lon_count - 1)], temp_send)
    save_next.wait()
    for g in range(groups):
        save(g).wait()


def in_hbm(array):
    return pltpu.with_memory_space_constraint(array, pltpu.HBM)


def store_kernel(parts, state, following, temp, state_out, following_out, temp_out, rows, sem):
    width = state.shape[0] // parts
    copies = [
        pltpu.make_async_copy(
            state.at[pl.ds(g * width, width)], state_out.at[pl.ds(g * width, width)], sem.at[g]
        )
        for g in range(parts)
    ]
    copies.append(pltpu.make_async_copy(following, following_out, sem.at[parts]))
    for copy in copies:
        copy.start()
    rows[:, :128] = temp[:, 0, :]
    rows[:, 128:] = temp[:, 1, :]
    copies.append(pltpu.make_async_copy(rows, temp_out, sem.at[parts + 1]))
    copies[-1].start()
    for copy in copies:
        copy.wait()


def store(state, following, temp):
    parts = 4
    rows = (temp.shape[0], temp.shape[1] * temp.shape[2])
    anywhere = pl.BlockSpec(memory_space=pl.ANY)
    return pl.pallas_call(
        functools.partial(store_kernel, parts),
        out_shape=(
            pltpu.HBM(state.shape, state.dtype),
            pltpu.HBM(following.shape, following.dtype),
            pltpu.HBM(rows, temp.dtype),
        ),
        in_specs=[anywhere, anywhere, pl.BlockSpec(memory_space=pltpu.VMEM)],
        out_specs=(anywhere,) * 3,
        scratch_shapes=[pltpu.VMEM(rows, temp.dtype), pltpu.SemaphoreType.DMA((parts + 2,))],
        compiler_params=pltpu.CompilerParams(vmem_limit_bytes=2 * 2**20),
        name="store_results",
    )(state, following, temp)


def coupled(
    cost_class, index, w_in, w_out, w_flux, atm_state, weight, tracers, land_sea
):
    sec_count, lon_count = lax.axis_size("sec"), lax.axis_size("lon")
    levels, ocean_rows, cells = tracers.shape[1:]
    blocks, feat = atm_state.shape[:2]
    hid = w_in.shape[0]
    longest, groups = 8, 2
    pairs = ocean_rows * 4
    fields = 2 * levels
    lines = fields * ocean_rows
    padded = -(-(lines + ocean_rows) // 128) * 128
    anywhere = pl.BlockSpec(memory_space=pl.ANY)
    hbm = pl.BlockSpec(memory_space=pltpu.HBM)
    smem = pl.BlockSpec(memory_space=pltpu.SMEM)
    vmem = pl.BlockSpec(memory_space=pltpu.VMEM)
    state, next_flat, temp = pl.pallas_call(
        functools.partial(coupled_kernel, sec_count, lon_count, levels, groups, longest),
        out_shape=(
            pltpu.VMEM(atm_state.shape, BF16),
            pltpu.VMEM((fields, ocean_rows, cells), F32),
            pltpu.VMEM((lon_count, 2, 128), F32),
        ),
        in_specs=[smem, smem, hbm, hbm, vmem, hbm, hbm, hbm, hbm],
        out_specs=(anywhere, anywhere, anywhere),
        scratch_shapes=[
            pltpu.VMEM((blocks, feat, cells), BF16),
            pltpu.VMEM((hid + 16, feat), BF16),
            pltpu.VMEM((feat, hid), BF16),
            pltpu.VMEM((hid, hid), BF16),
            pltpu.VMEM((16, hid), BF16),
            pltpu.VMEM((lon_count, 4, cells), F32),
            pltpu.SemaphoreType.DMA((groups,)),
            pltpu.SemaphoreType.DMA((groups,)),
            pltpu.SemaphoreType.DMA((2,)),
            pltpu.VMEM((pairs, cells, cells), BF16),
            pltpu.VMEM((fields, ocean_rows, cells), F32),
            pltpu.VMEM((ocean_rows, cells), jnp.int32),
            pltpu.VMEM((fields, ocean_rows, cells), F32),
            pltpu.VMEM((lon_count, 4, cells), F32),
            pltpu.VMEM((128, cells), F32),
            pltpu.VMEM((lon_count, 2, 128), F32),
            pltpu.VMEM((padded, cells), BF16),
            pltpu.VMEM((8, padded), F32),
            pltpu.VMEM((8, padded), F32),
            pltpu.VMEM((8, padded), F32),
            pltpu.VMEM((padded, cells), F32),
            pltpu.VMEM((fields + 16, cells), BF16),
            pltpu.VMEM((fields + 16, cells), BF16),
            pltpu.VMEM((fields + 16, cells), F32),
            pltpu.SemaphoreType.DMA((pairs // 8,)),
            pltpu.SemaphoreType.DMA,
            pltpu.SemaphoreType.DMA,
            pltpu.SemaphoreType.DMA,
            pltpu.SemaphoreType.DMA,
            pltpu.SemaphoreType.DMA,
            pltpu.SemaphoreType.DMA,
            pltpu.SemaphoreType.DMA,
            pltpu.SemaphoreType.DMA((3,)),
            pltpu.SemaphoreType.DMA((3,)),
        ]
        + [pltpu.VMEM((hid, cells), F32)] * blocks
        + [pltpu.VMEM((hid, cells), BF16)] * (2 * blocks),
        compiler_params=pltpu.CompilerParams(
            vmem_limit_bytes=50 * 2**20, collective_id=0, has_side_effects=True
        ),
        name="coupled_step",
    )(
        cost_class,
        index[:, 0].T,
        in_hbm(w_in),
        in_hbm(w_out),
        w_flux,
        in_hbm(atm_state),
        in_hbm(weight.reshape(pairs, cells, cells)),
        in_hbm(tracers.reshape(fields, ocean_rows, cells)),
        in_hbm(land_sea),
    )
    state, next_flat, temp = store(state, next_flat, temp)
    return state, next_flat.reshape(tracers.shape), temp


def per_device(
    atm_state,
    cost_class,
    w_in,
    w_out,
    w_flux,
    feeding_block_index,
    pairwise_remap_weight,
    ocean_tracers,
    land_sea,
):
    return coupled(
        cost_class,
        feeding_block_index,
        w_in,
        w_out,
        w_flux,
        atm_state,
        pairwise_remap_weight,
        ocean_tracers,
        land_sea,
    )


def solution(mesh):
    return jax.shard_map(
        per_device,
        mesh=mesh,
        in_specs=(
            P(("sec", "lon", "lat"), None, None),
            P(("sec", "lon", "lat")),
            P(),
            P(),
            P(),
            P("lat", ("sec", "lon"), None),
            P("lat", ("sec", "lon"), None, None, None),
            P(None, None, "lat", ("sec", "lon")),
            P("lat", ("sec", "lon")),
        ),
        out_specs=(
            P(("sec", "lon", "lat"), None, None),
            P(None, None, "lat", ("sec", "lon")),
            P(("sec", "lon", "lat"), None),
        ),
        check_vma=False,
    )
```
